256 devices in a mesh: enc: 8 (over y, core), exp: 32 (over x, z).
Axes of the slice: x: 4, y: 4, z: 8, core: 2. Of those that a mesh axis runs over, the one named last changes fastest.
Arguments:
- tokens: bfloat16 [4096, 4096], P('exp'), may hold values from -61 to 61
- norm_gain: bfloat16 [4096], replicated, may hold values from 0.099609375 to 1.8984375
- router: bfloat16 [64, 4096], replicated, may hold values from -0.09375 to 0.09375
- routes: int32 [4096, 8], P('exp'), may hold values from 0 to 63, all different within a row; in each aligned block of 128 rows (0 to 127, 128 to 255, ...) at most 32 rows name the same one
- w_gate: bfloat16 [64, 1536, 4096], P('exp', 'enc'), may hold values from -0.09375 to 0.09375
- w_up: bfloat16 [64, 1536, 4096], P('exp', 'enc'), may hold values from -0.09375 to 0.09375
- w_down: bfloat16 [64, 1536, 4096], P('exp', None, 'enc'), may hold values from -0.15625 to 0.15625
Outputs:
- mixed: bfloat16 [4096, 4096], P('exp', 'enc')
The draws below stay inside these ranges and needn't reach their ends.
Inputs may be any that keep to these rules, and one draw needn't show every extreme that they name: `routes`: each row names 8 different experts. In the rows of one owner (128 rows, aligned), no expert is named more than 32 times, a bound that some block reaches.
All inputs are finite; a program needn't handle non-finite values.
Results may differ from the reference program's by a relative error of at most 0.024.
Values may be sent and summed in bfloat16 or wider, within the bound.
No kernel may reach another device: no remote copies, remote signals or barrier semaphores. Data moves between devices by JAX's collectives and lax.ppermute only.
A program may use at most 128 MiB of HBM per device.

```python
import math
import jax
import jax.numpy as jnp
import numpy as np
from jax import lax

D = 4096
FF = 1536
TOPK = 8
TOK_OWN = 128
EXPERTS = 64
TOKENS = 4096
CAP = 32
N_EXP = 32


def draw_tokens(key, part):
    key = jax.random.fold_in(key, 11)
    key_base, key_rows, key_cols = jax.random.split(key, 3)
    raw_values = jax.random.truncated_normal(key_base, -4.0, 4.0, (TOKENS, D), jnp.float32)
    row_scale = jnp.exp(jax.random.uniform(key_rows, (TOKENS, 1), jnp.float32, math.log(0.3), math.log(3.0)))
    col_scale = jnp.exp(jax.random.uniform(key_cols, (1, D), jnp.float32, math.log(0.5), math.log(5.0)))
    return (raw_values * row_scale * col_scale).astype(jnp.bfloat16)


def steps_of(key, shape, shards, smallest, largest):
    def one(position, blocks):
        steps = jax.random.uniform(jax.random.fold_in(jax.random.fold_in(key, 6), position), (blocks,), jnp.float32, smallest / len(shards), largest / len(shards))
        return jnp.repeat(jnp.exp(steps), shape[position] // blocks).reshape((-1,) + (1,) * (len(shape) - position - 1))

    level = one(*shards[0])
    for cut in shards[1:]:
        level = level * one(*cut)
    return level


def assign_block(rng, own, number, rows, count, top, limit, slope):
    sequence = jax.random.permutation(rng, count)
    heavy_load, common = shares(count, rows * top, limit, slope, True), shares(count, rows * top, limit, slope, False)
    places = jnp.arange(count)

    def named(lengths, offset_by):
        used = int((lengths > 0).sum())
        fixed = max(1, used // 4)
        moved = fixed + (places - fixed + offset_by * (used - fixed)) % max(1, count - fixed)
        return jnp.zeros((count,), jnp.int32).at[sequence[jnp.where(places < fixed, places, moved)]].set(jnp.asarray(lengths, jnp.int32))

    lengths = jnp.where(number % 4 == 0, named(heavy_load, number // 4), named(common, number - number // 4 - 1))
    mixed = jax.random.permutation(jax.random.fold_in(own, 3), count)
    giver, sink = mixed[0:count // 2 * 2:2], mixed[1:count // 2 * 2:2]
    slack = jnp.minimum(lengths[giver] - 1, limit - lengths[sink]) // 2
    slack = jnp.where((giver == sequence[0]) | (sink == sequence[0]) | (lengths[sink] == 0), 0, jnp.maximum(slack, 0))
    moved = jax.random.randint(jax.random.fold_in(own, 4), (count // 2,), 0, 1 << 20) % (slack + 1)
    lengths = lengths.at[giver].add(-moved).at[sink].add(moved)
    members = jnp.searchsorted(jnp.cumsum(lengths), jnp.arange(rows * top), side="right").astype(jnp.int32)
    table = members.reshape(top, rows).T
    table = table[jax.random.permutation(jax.random.fold_in(own, 1), rows)]
    offset_by = jax.random.randint(jax.random.fold_in(own, 2), (rows, 1), 0, top)
    return jnp.take_along_axis(table, (jnp.arange(top)[None, :] + offset_by) % top, axis=1)


def shares(amount, total, reach, lean, full):
    weights = [(1 << 20) // math.isqrt(grade ** lean) + 1 for grade in range(1, amount + 1)]
    largest = reach if full else min(reach, max(-(-total // amount), total * weights[0] // sum(weights)))
    least = 1 if total - largest >= amount - 1 else 0
    given, rest = [largest] + [least] * (amount - 1), total - largest - least * (amount - 1)
    while rest > 0:
        free = [i for i in range(1, amount) if given[i] < largest] or [i for i in range(1, amount) if given[i] < reach]
        whole, budget = sum([weights[i] for i in free]), rest
        for i in free:
            extra = min(reach - given[i], max(1, budget * weights[i] // whole), rest)
            given[i] = given[i] + extra
            rest = rest - extra
    return np.array(given)


def gaussian(key, shape, width, reach, cuts=(), kind=jnp.bfloat16):
    drawn = jax.random.normal(key, shape, jnp.float32) * width
    if len(cuts) > 0:
        drawn = steps_of(key, shape, cuts, -0.22, 0.18) * drawn
    return jnp.clip(drawn, min=-reach, max=reach).astype(kind)


def setup_inputs(seed: int = 0) -> dict:
    key_of = jax.random.split(jax.random.key(seed), 8)
    tokens = draw_tokens(jax.random.fold_in(key_of[7], 71), 0)
    norm_gain = jnp.clip(1.0 + 0.18 * jax.random.normal(key_of[1], (D,), jnp.float32), 0.099609375, 1.8984375).astype(jnp.bfloat16)
    router = gaussian(key_of[2], (EXPERTS, D), D ** -0.5, 0.09375)
    routes_keys = jax.random.split(jax.random.fold_in(key_of[3], 1), TOKENS // TOK_OWN)
    routes_turns = jax.random.permutation(jax.random.fold_in(key_of[3], 3), TOKENS // TOK_OWN)
    routes = jax.vmap(lambda own, number: assign_block(jax.random.fold_in(key_of[3], 2), own, number, TOK_OWN, EXPERTS, TOPK, CAP, 2))(routes_keys, routes_turns).reshape((TOKENS, TOPK))
    w_gate = gaussian(key_of[4], (EXPERTS, FF, D), D ** -0.5, 0.09375, ((0, 32), (1, 8)))
    w_up = gaussian(key_of[5], (EXPERTS, FF, D), D ** -0.5, 0.09375, ((0, 32), (1, 8)))
    w_down = gaussian(key_of[6], (EXPERTS, FF, D), FF ** -0.5, 0.15625, ((0, 32), (2, 8)))
    return {"tokens": tokens, "norm_gain": norm_gain, "router": router, "routes": routes, "w_gate": w_gate, "w_up": w_up, "w_down": w_down}


EPS = 1e-06

def by_rows(left, right):
    return lax.dot_general(left, right, (((1,), (1,)), ((), ())), preferred_element_type=jnp.float32)

def reference(tokens, norm_gain, router, routes, w_gate, w_up, w_down):
    values = tokens.astype(jnp.float32)
    scaled = (values * norm_gain.astype(jnp.float32)).astype(jnp.bfloat16)
    squares = lax.optimization_barrier(jnp.sum(values * values, axis=1, keepdims=True))
    inverse = lax.rsqrt(squares / D + EPS)
    logits = by_rows(scaled, router) * inverse
    normed = (scaled.astype(jnp.float32) * inverse).astype(jnp.bfloat16)
    chosen_mask = routes[:, :, None] == jnp.arange(EXPERTS, dtype=jnp.int32)
    chosen = lax.optimization_barrier(jnp.sum(jnp.where(chosen_mask, logits[:, None, :], 0.0), axis=2))
    raised = jnp.exp(chosen)
    weights = raised / lax.optimization_barrier(jnp.sum(raised, axis=1, keepdims=True))
    owner_ids = (jnp.arange(TOKENS, dtype=jnp.int32) // TOK_OWN).astype(jnp.int32)
    slot_total = N_EXP * CAP

    def one_expert(running, inputs):
        expert_id, gate_w, up_w, down_w = inputs
        hit_pairs = routes == expert_id
        hit_rows = jnp.any(hit_pairs, axis=1)
        hit_count = hit_rows.astype(jnp.int32).reshape(N_EXP, TOK_OWN)
        ranking = (jnp.cumsum(hit_count, axis=1) - hit_count).reshape(-1).astype(jnp.int32)
        slot_index = jnp.where(hit_rows, owner_ids * CAP + ranking, slot_total).astype(jnp.int32)
        slot_rows = jnp.zeros((slot_total, D), jnp.bfloat16).at[slot_index].set(normed, mode='drop')
        gate_sum = by_rows(slot_rows, gate_w)
        up_sum = by_rows(slot_rows, up_w)
        hidden = (jax.nn.silu(gate_sum) * up_sum).astype(jnp.bfloat16)
        expert_out = jnp.dot(hidden, down_w, preferred_element_type=jnp.float32).astype(jnp.bfloat16)
        share = lax.optimization_barrier(jnp.sum(jnp.where(hit_pairs, weights, 0.0), axis=1))
        picked = expert_out[jnp.minimum(slot_index, slot_total - 1)].astype(jnp.float32)
        return (running + share[:, None] * picked, None)
    running, _ = lax.scan(one_expert, jnp.zeros((TOKENS, D), jnp.float32), (jnp.arange(EXPERTS, dtype=jnp.int32), w_gate, w_up, w_down))
    return running.astype(jnp.bfloat16)
```

```python
import jax
import jax.numpy as jnp
from jax import lax
from jax.sharding import PartitionSpec as P

EPS = 1e-06


def by_rows(left, right):
    return lax.dot_general(
        left, right, (((1,), (1,)), ((), ())), preferred_element_type=jnp.float32
    )


def body(tokens, norm_gain, router, routes, w_gate, w_up, w_down):
    tok_rows, width = tokens.shape
    experts = router.shape[0]
    top_count = routes.shape[1]
    exp_local = w_gate.shape[0]
    out_cols = w_down.shape[2]
    n_exp = experts // exp_local
    capacity = 2 * tok_rows * top_count // experts
    values = tokens.astype(jnp.float32)
    scaled = (values * norm_gain.astype(jnp.float32)).astype(jnp.bfloat16)
    squares = jnp.sum(values * values, axis=1, keepdims=True)
    inverse = lax.rsqrt(squares / width + EPS)
    start = lax.axis_index("enc") * out_cols
    part = lax.dynamic_slice(scaled, (0, start), (tok_rows, out_cols))
    normed = (part.astype(jnp.float32) * inverse).astype(jnp.bfloat16)

    routes_t = routes.T
    labels = lax.broadcasted_iota(jnp.int32, (experts, 1, 1), 0)
    chosen_t = routes_t[None] == labels
    mask_t = jnp.any(chosen_t, axis=1)
    row = lax.broadcasted_iota(jnp.int32, (tok_rows, tok_rows), 0)
    col = lax.broadcasted_iota(jnp.int32, (tok_rows, tok_rows), 1)
    earlier = (row < col).astype(jnp.bfloat16)
    before = jnp.dot(
        mask_t.astype(jnp.bfloat16), earlier, preferred_element_type=jnp.float32
    ).astype(jnp.int32)
    place = jnp.where(mask_t, before, -1)
    slots = lax.broadcasted_iota(jnp.int32, (1, capacity, 1), 1)
    select = place[:, None, :] == slots
    pick = select.astype(jnp.bfloat16).reshape(n_exp, exp_local, capacity, tok_rows)

    received = []
    for member in range(exp_local):
        rows = jnp.dot(
            pick[:, member].reshape(n_exp * capacity, tok_rows),
            normed,
            preferred_element_type=jnp.float32,
        ).astype(jnp.bfloat16)
        received.append(
            lax.all_to_all(rows, "exp", split_axis=0, concat_axis=0, tiled=True)
        )

    logits = by_rows(scaled, router) * inverse
    logits_t = logits.T
    chosen = jnp.sum(jnp.where(chosen_t, logits_t[:, None, :], 0.0), axis=0)
    raised = jnp.exp(chosen)
    weights = raised / jnp.sum(raised, axis=0, keepdims=True)
    dense = jnp.sum(jnp.where(chosen_t, weights[None], 0.0), axis=1)
    mix = jnp.where(select, dense[:, None, :], 0.0).astype(jnp.bfloat16)
    mix = mix.reshape(n_exp, exp_local, capacity, tok_rows)

    total = None
    for member in range(exp_local):
        slot_rows = lax.all_gather(received[member], "enc", axis=1, tiled=True)
        gate_part = by_rows(slot_rows, w_gate[member])
        up_part = by_rows(slot_rows, w_up[member])
        hidden = (jax.nn.silu(gate_part) * up_part).astype(jnp.bfloat16)
        full = lax.all_gather(hidden, "enc", axis=1, tiled=True)
        result = jnp.dot(full, w_down[member], preferred_element_type=jnp.float32)
        back = lax.all_to_all(
            result.astype(jnp.bfloat16), "exp", split_axis=0, concat_axis=0, tiled=True
        )
        share = lax.dot_general(
            mix[:, member].reshape(n_exp * capacity, tok_rows),
            back,
            (((0,), (0,)), ((), ())),
            preferred_element_type=jnp.float32,
        )
        total = share if total is None else total + share
    return total.astype(jnp.bfloat16)


def solution(mesh):
    return jax.shard_map(
        body,
        mesh=mesh,
        in_specs=(
            P("exp", None),
            P(),
            P(),
            P("exp", None),
            P("exp", "enc", None),
            P("exp", "enc", None),
            P("exp", None, "enc"),
        ),
        out_specs=P("exp", "enc"),
        check_vma=False,
    )
```

```python
import jax
import jax.numpy as jnp
from jax import lax
from jax.experimental import pallas as pl
from jax.experimental.pallas import tpu as pltpu
from jax.sharding import Mesh, PartitionSpec as P

EPS = 1e-06
F32 = jnp.float32
BF16 = jnp.bfloat16
NY, NC, NX, NZ = 4, 2, 4, 8
ORDER = (0, 2, 3, 1)
SLOTS = 32

VMEM = pl.BlockSpec(memory_space=pltpu.VMEM)
SMEM = pl.BlockSpec(memory_space=pltpu.SMEM)


def by_rows(left, right):
    return lax.dot_general(
        left, right, (((1,), (1,)), ((), ())), preferred_element_type=F32
    )


def times(left, right):
    return jnp.dot(left, right, preferred_element_type=F32)


def call(kernel, outs, args, flops, moved, vmem=48):
    return pl.pallas_call(
        kernel,
        out_shape=outs,
        in_specs=[SMEM] + [VMEM] * (len(args) - 1),
        out_specs=jax.tree.map(lambda _: VMEM, outs),
        compiler_params=pltpu.CompilerParams(vmem_limit_bytes=vmem << 20),
        cost_estimate=pl.CostEstimate(
            flops=flops, bytes_accessed=moved, transcendentals=0
        ),
    )(*args)


def places(info, pos):
    tokens = info.shape[1]
    first = (2 * NZ * pos[0] + pos[3]).astype(F32)
    expert = first + 2.0 * lax.broadcasted_iota(jnp.int32, (NZ, tokens), 0).astype(F32)
    hits = [info[k : k + 1, :] == expert for k in range(8)]
    named = hits[0]
    for hit in hits[1:]:
        named = named | hit
    row = lax.broadcasted_iota(jnp.int32, (tokens, tokens), 0)
    col = lax.broadcasted_iota(jnp.int32, (tokens, tokens), 1)
    earlier = jnp.where(row < col, 1.0, 0.0).astype(BF16)
    before = times(jnp.where(named, 1.0, 0.0).astype(BF16), earlier)
    return hits, jnp.where(named, before, -1.0)


def spread(place, values):
    tokens = place.shape[1]
    slot = lax.broadcasted_iota(jnp.int32, (SLOTS, tokens), 0).astype(F32)
    return jnp.concatenate(
        [
            jnp.where(place[z : z + 1, :] == slot, values[z : z + 1, :], 0.0)
            for z in range(NZ)
        ],
        axis=0,
    )


def select(info, part, pos):
    _, place = places(info, pos)
    picks = spread(place, jnp.ones_like(place)).astype(BF16)
    return times(picks, part).astype(BF16)


def prepare_kernel(pos, tokens, gain, router, routes, part_out, rows_out, info_out):
    values = tokens[...].astype(F32)
    width = values.shape[1]
    count = values.shape[0]
    scaled = (values * gain[...].astype(F32)).astype(BF16)
    squares = jnp.sum(values * values, axis=1, keepdims=True)
    inverse = lax.rsqrt(squares / width + EPS)
    quarter = width // NY
    at = pl.multiple_of(pos[1] * quarter, quarter)
    mine = (tokens[:, pl.ds(at, quarter)].astype(F32) * gain[:, pl.ds(at, quarter)].astype(F32)).astype(BF16)
    part = (mine.astype(F32) * inverse).astype(BF16)
    part_out[...] = part
    turned = jnp.transpose(jnp.broadcast_to(inverse, (count, 128)))
    logits = by_rows(router[...], scaled) * turned[0:1, :]
    expert = lax.broadcasted_iota(jnp.int32, logits.shape, 0).astype(F32)
    names = routes[...].astype(F32)
    chosen = [
        jnp.sum(jnp.where(names[k : k + 1, :] == expert, logits, 0.0), axis=0, keepdims=True)
        for k in range(8)
    ]
    raised = jnp.exp(jnp.concatenate(chosen, axis=0))
    weights = raised / jnp.sum(raised, axis=0, keepdims=True)
    info_out[0:8, :] = names
    info_out[8:16, :] = weights
    rows_out[...] = select(names, part, pos)


def select_kernel(pos, part, info, rows_out):
    rows_out[...] = select(info[0:8, :], part[...], pos)


def hidden_kernel(pos, own, low, high, far_top, far_bottom, w_gate, w_up, out):
    quarter = own.shape[1]
    far = jnp.concatenate([far_top[...], far_bottom[...]], axis=0)
    gate = up = None
    for block, shift in ((own[...], 0), (low[...], 3), (high[...], 1), (far, 2)):
        index = lax.rem(pos[1] + shift, NY)
        cols = pl.ds(pl.multiple_of(index * quarter, quarter), quarter)
        gate_step = by_rows(block, w_gate[:, cols])
        up_step = by_rows(block, w_up[:, cols])
        gate = gate_step if gate is None else gate + gate_step
        up = up_step if up is None else up + up_step
    out[...] = (gate / (1.0 + jnp.exp(-gate)) * up).astype(BF16)


def down_kernel(pos, own, low, high, far_top, far_bottom, w_down, out):
    units = own.shape[1]
    cols = w_down.shape[2]
    far = jnp.concatenate([far_top[...], far_bottom[...]], axis=0)
    for core in range(NC):
        total = None
        for block, shift in ((own[...], 0), (low[...], 3), (high[...], 1), (far, 2)):
            index = lax.rem(pos[1] + shift, NY)
            rows = pl.ds(pl.multiple_of(index * units, units), units)
            step = times(block, w_down[core, rows, :])
            total = step if total is None else total + step
        out[:, core * cols : (core + 1) * cols] = total.astype(BF16)


def combine_kernel(pos, info, rows, keep_out, give_out):
    hits, place = places(info[0:8, :], pos)
    dense = jnp.zeros_like(place)
    for k in range(8):
        dense = dense + jnp.where(hits[k], info[8 + k : 9 + k, :], 0.0)
    mix = jnp.transpose(spread(place, dense)).astype(BF16)
    cols = keep_out.shape[1]
    mine = pl.ds(pl.multiple_of(pos[3] * cols, cols), cols)
    other = pl.ds(pl.multiple_of((1 - pos[3]) * cols, cols), cols)
    keep_out[...] = times(mix, rows[:, mine]).astype(BF16)
    give_out[...] = times(mix, rows[:, other]).astype(BF16)


def shift(array, axis, step, size):
    return lax.ppermute(array, axis, [(i, (i + step) % size) for i in range(size)])


def ring(block):
    half = block.shape[0] // 2
    low = shift(block, "y", 1, NY)
    high = shift(block, "y", -1, NY)
    far_top = shift(low[:half], "y", 1, NY)
    far_bottom = shift(high[half:], "y", -1, NY)
    return block, low, high, far_top, far_bottom


def body(tokens, norm_gain, router, routes, w_gate, w_up, w_down):
    count, width = tokens.shape
    quarter = width // NY
    units = 2 * w_gate.shape[1]
    ff = w_down.shape[1]
    cols = w_down.shape[2]
    rows = NZ * SLOTS
    sds = jax.ShapeDtypeStruct
    pos = jnp.stack(
        [lax.axis_index("x"), lax.axis_index("y"), lax.axis_index("z"), lax.axis_index("c")]
    ).astype(jnp.int32)

    part, first_rows, info = call(
        prepare_kernel,
        (sds((count, quarter), BF16), sds((rows, quarter), BF16), sds((16, count), F32)),
        (pos, tokens, norm_gain[None, :], router, routes.T),
        2 * count * width * 64 + 2 * rows * count * quarter,
        count * width * 2,
    )
    parts, infos, dispatched = {0: part}, {0: info}, {0: first_rows}
    for step in (1, 3, 2):
        infos[step] = shift(info, "x", step, NX)
        parts[step] = shift(part, "x", step, NX)
    own_gate = lax.all_to_all(w_gate, "c", 0, 0, tiled=True).reshape(units, width)
    own_up = lax.all_to_all(w_up, "c", 0, 0, tiled=True).reshape(units, width)
    own_down = lax.all_to_all(w_down, "c", 0, 0, tiled=True)

    total = None
    for step in ORDER:
        if step:
            picked = call(
                select_kernel,
                sds((rows, quarter), BF16),
                (pos, parts[step], infos[step]),
                2 * rows * count * quarter,
                rows * quarter * 2,
            )
        else:
            picked = first_rows
        mine = lax.all_to_all(picked, "z", 0, 0, tiled=True)
        hidden = call(
            hidden_kernel,
            sds((rows, units), BF16),
            (pos, *ring(mine), own_gate, own_up),
            4 * rows * width * units,
            4 * units * width + 2 * rows * width,
        )
        result = call(
            down_kernel,
            sds((rows, NC * cols), BF16),
            (pos, *ring(hidden), own_down),
            2 * rows * ff * NC * cols,
            2 * ff * NC * cols + 2 * rows * NC * cols,
        )
        back = lax.all_to_all(result, "z", 0, 0, tiled=True)
        keep, give = call(
            combine_kernel,
            (sds((count, cols), BF16), sds((count, cols), BF16)),
            (pos, infos[step], back),
            2 * rows * count * NC * cols,
            2 * rows * NC * cols,
        )
        if step:
            keep = shift(keep, "x", -step, NX)
        pairs = [
            (core * NX + i, (1 - core) * NX + (i - step) % NX)
            for core in range(NC)
            for i in range(NX)
        ]
        give = lax.ppermute(give, ("c", "x"), pairs)
        share = keep.astype(F32) + give.astype(F32)
        total = share if total is None else total + share
    return total.astype(BF16)


def solution(mesh):
    grid = Mesh(mesh.devices.reshape(NY, NC, NX, NZ), ("y", "c", "x", "z"))
    enc, exp = ("y", "c"), ("x", "z")
    return jax.shard_map(
        body,
        mesh=grid,
        in_specs=(
            P(exp, None),
            P(),
            P(),
            P(exp, None),
            P(exp, enc, None),
            P(exp, enc, None),
            P(exp, None, enc),
        ),
        out_specs=P(exp, enc),
        check_vma=False,
    )
```

```python
import functools

import jax
import jax.numpy as jnp
from jax import lax
from jax.experimental import pallas as pl
from jax.experimental.pallas import tpu as pltpu
from jax.sharding import Mesh, PartitionSpec as P

EPS = 1e-06
F32 = jnp.float32
BF16 = jnp.bfloat16
NY, NC, NX, NZ = 4, 2, 4, 8
N_EXP = NX * NZ
CHUNKS = ((0, 8), (8, 16), (24, 8))
PIECE = 256

VMEM = pl.BlockSpec(memory_space=pltpu.VMEM)
SMEM = pl.BlockSpec(memory_space=pltpu.SMEM)


def by_rows(left, right):
    return lax.dot_general(
        left, right, (((1,), (1,)), ((), ())), preferred_element_type=F32
    )


def times(left, right):
    return jnp.dot(left, right, preferred_element_type=F32)


def params(mib):
    return pltpu.CompilerParams(vmem_limit_bytes=mib << 20)


def cost(flops, moved):
    return pl.CostEstimate(flops=flops, bytes_accessed=moved, transcendentals=0)


def places(names, core):
    tokens = names.shape[1]
    expert = core.astype(F32) + 2.0 * lax.broadcasted_iota(
        jnp.int32, (N_EXP, tokens), 0
    ).astype(F32)
    hits = [names[k : k + 1, :] == expert for k in range(8)]
    named = hits[0]
    for hit in hits[1:]:
        named = named | hit
    row = lax.broadcasted_iota(jnp.int32, (tokens, tokens), 0)
    col = lax.broadcasted_iota(jnp.int32, (tokens, tokens), 1)
    earlier = jnp.where(row < col, 1.0, 0.0).astype(BF16)
    before = times(jnp.where(named, 1.0, 0.0).astype(BF16), earlier)
    return hits, jnp.where(named, before, -1.0)


def spread(place, values, first, size):
    tokens = place.shape[1]
    slot = lax.broadcasted_iota(jnp.int32, (size, tokens), 0) + first
    slot = slot.astype(F32)
    return jnp.concatenate(
        [
            jnp.where(place[d : d + 1, :] == slot, values[d : d + 1, :], 0.0)
            for d in range(N_EXP)
        ],
        axis=0,
    )


def pick(names, part, chunk, core):
    _, place = places(names, core)
    picks = spread(place, jnp.ones_like(place), *chunk).astype(BF16)
    return times(picks, part).astype(BF16)


def first_kernel(pos, tokens, gain, routes, part_out, rows_out):
    values = tokens[...].astype(F32)
    count, width = values.shape
    squares = jnp.sum(values * values, axis=1, keepdims=True)
    inverse = lax.rsqrt(squares / width + EPS)
    quarter = width // NY
    cols = pl.ds(pl.multiple_of(pos[0] * quarter, quarter), quarter)
    mine = (tokens[:, cols].astype(F32) * gain[:, cols].astype(F32)).astype(BF16)
    part = (mine.astype(F32) * inverse).astype(BF16)
    part_out[...] = part
    rows_out[...] = pick(routes[...].astype(F32), part, CHUNKS[0], pos[1])


def later_kernel(pos, part, routes, *rows_out):
    for chunk, out in zip(CHUNKS[1:], rows_out):
        out[...] = pick(routes[...].astype(F32), part[...], chunk, pos[1])


def mix_kernel(pos, tokens, gain, router, routes, *mix_out):
    values = tokens[...].astype(F32)
    count, width = values.shape
    scaled = (values * gain[...].astype(F32)).astype(BF16)
    squares = jnp.sum(values * values, axis=1, keepdims=True)
    inverse = lax.rsqrt(squares / width + EPS)
    turned = jnp.transpose(jnp.broadcast_to(inverse, (count, 128)))
    logits = by_rows(router[...], scaled) * turned[0:1, :]
    expert = lax.broadcasted_iota(jnp.int32, logits.shape, 0).astype(F32)
    names = routes[...].astype(F32)
    chosen = [
        jnp.sum(jnp.where(names[k : k + 1, :] == expert, logits, 0.0), axis=0, keepdims=True)
        for k in range(8)
    ]
    raised = jnp.exp(jnp.concatenate(chosen, axis=0))
    weights = raised / jnp.sum(raised, axis=0, keepdims=True)
    hits, place = places(names, pos[1])
    dense = jnp.zeros_like(place)
    for k in range(8):
        dense = dense + jnp.where(hits[k], weights[k : k + 1, :], 0.0)
    for (first, size), out in zip(CHUNKS, mix_out):
        out[...] = jnp.transpose(spread(place, dense, first, size)).astype(BF16)


def hidden_kernel(pos, blocks, gate_own, gate_other, up_own, up_other, out):
    quarter = blocks.shape[2]
    sums = [None] * 4
    for index in range(NY):
        block = blocks[index]
        cols = slice(index * quarter, (index + 1) * quarter)
        for which, rows in enumerate(
            (gate_own[0, :, cols], up_own[0, :, cols], gate_other[:, cols], up_other[:, cols])
        ):
            step = by_rows(block, rows)
            sums[which] = step if sums[which] is None else sums[which] + step
    own, other = [
        gate / (1.0 + jnp.exp(-gate)) * up for gate, up in (sums[0:2], sums[2:4])
    ]
    low = jnp.where(pos[1] == 0, own, other)
    high = jnp.where(pos[1] == 0, other, own)
    out[...] = jnp.concatenate([low, high], axis=1).astype(BF16)


def down_kernel(pos, down_own, down_other, *refs):
    out = refs[-1]
    cols = down_other.shape[1]
    for index, blocks in enumerate(refs[:-1]):
        rows, units = blocks.shape[1:]
        at = slice(index * rows, (index + 1) * rows)
        own = other = None
        for y in range(NY):
            span = slice(y * units, (y + 1) * units)
            own_step = times(blocks[y], down_own[0, span, :])
            other_step = times(blocks[y], down_other[span, :])
            own = own_step if own is None else own + own_step
            other = other_step if other is None else other + other_step
        for core, total in ((pos[1], own), (1 - pos[1], other)):
            out[at, pl.ds(pl.multiple_of(core * cols, cols), cols)] = total.astype(BF16)


def combine_kernel(pos, *refs):
    keep_out, give_out = refs[-2:]
    cols = keep_out.shape[1]
    pairs = len(refs) // 2 - 1
    for out, core in ((give_out, 1 - pos[1]), (keep_out, pos[1])):
        at = pl.ds(pl.multiple_of(core * cols, cols), cols)
        total = None
        for index in range(pairs):
            step = times(refs[2 * index][...], refs[2 * index + 1][:, at])
            total = step if total is None else total + step
        out[...] = total.astype(out.dtype)


def body(tokens, norm_gain, router, routes, w_gate, w_up, w_down):
    count, width = tokens.shape
    quarter = width // NY
    units = 2 * w_gate.shape[1]
    ff = w_down.shape[1]
    cols = w_down.shape[2]
    sds = jax.ShapeDtypeStruct
    pos = jnp.stack([lax.axis_index("y"), lax.axis_index("c")]).astype(jnp.int32)
    turned = routes.T
    sizes = [N_EXP * size for _, size in CHUNKS]

    gain = norm_gain[None, :]
    part, first_rows = pl.pallas_call(
        first_kernel,
        out_shape=(sds((count, quarter), BF16), sds((sizes[0], quarter), BF16)),
        in_specs=[SMEM] + [VMEM] * 3,
        out_specs=(VMEM, VMEM),
        compiler_params=params(16),
        cost_estimate=cost(2 * count * sizes[0] * quarter, count * width * 2),
    )(pos, tokens, gain, turned)
    received = [lax.all_to_all(first_rows, ("x", "z"), 0, 0, tiled=True)]
    later_rows = pl.pallas_call(
        later_kernel,
        out_shape=tuple(sds((size, quarter), BF16) for size in sizes[1:]),
        in_specs=[SMEM] + [VMEM] * 2,
        out_specs=(VMEM,) * (len(CHUNKS) - 1),
        compiler_params=params(16),
        cost_estimate=cost(2 * count * sum(sizes) * quarter, sum(sizes) * quarter * 2),
    )(pos, part, turned)
    sent = [
        lax.dynamic_index_in_dim(array, 1 - pos[1], 0, keepdims=False)
        for array in (w_gate, w_up, w_down)
    ]
    *sent, received[0] = lax.optimization_barrier((*sent, received[0]))
    others = [lax.ppermute(array, "c", [(0, 1), (1, 0)]) for array in sent]
    for rows in later_rows:
        rows, received[-1] = lax.optimization_barrier((rows, received[-1]))
        received.append(lax.all_to_all(rows, ("x", "z"), 0, 0, tiled=True))
    tokens, router, received[0] = lax.optimization_barrier((tokens, router, received[0]))
    mixes = pl.pallas_call(
        mix_kernel,
        out_shape=tuple(sds((count, size), BF16) for size in sizes),
        in_specs=[SMEM] + [VMEM] * 4,
        out_specs=(VMEM,) * len(CHUNKS),
        compiler_params=params(16),
        cost_estimate=cost(2 * count * width * 64, count * width * 2),
    )(pos, tokens, gain, router, turned)

    returned = []
    done = []
    for index, size in enumerate(sizes):
        mine = received[index]
        if index:
            before = [done[i][j] for i, j in ((index - 1, 0), (index - 2, 1)) if i >= 0]
            mine, *before = lax.optimization_barrier((mine, *before))
        blocks = lax.all_gather(mine, "y", axis=0)
        pieces = []
        for half in range(size // PIECE):
            hidden = pl.pallas_call(
                hidden_kernel,
                grid_spec=pltpu.PrefetchScalarGridSpec(
                    num_scalar_prefetch=1,
                    grid=(1,),
                    in_specs=[
                        pl.BlockSpec(
                            (NY, PIECE, quarter), lambda step, pos, half=half: (0, half, 0)
                        ),
                        pl.BlockSpec((1, units // 2, width), lambda step, pos: (pos[1], 0, 0)),
                        pl.BlockSpec((units // 2, width), lambda step, pos: (0, 0)),
                        pl.BlockSpec((1, units // 2, width), lambda step, pos: (pos[1], 0, 0)),
                        pl.BlockSpec((units // 2, width), lambda step, pos: (0, 0)),
                    ],
                    out_specs=pl.BlockSpec((PIECE, units), lambda step, pos: (0, 0)),
                ),
                out_shape=sds((PIECE, units), BF16),
                compiler_params=params(32),
                cost_estimate=cost(
                    4 * PIECE * width * units, 4 * units * width + 2 * PIECE * width
                ),
            )(pos, blocks, w_gate, others[0], w_up, others[1])
            pieces.append(lax.all_gather(hidden, "y", axis=0))
        result = pl.pallas_call(
            down_kernel,
            grid_spec=pltpu.PrefetchScalarGridSpec(
                num_scalar_prefetch=1,
                grid=(1,),
                in_specs=[
                    pl.BlockSpec((1, ff, cols), lambda step, pos: (pos[1], 0, 0)),
                    pl.BlockSpec((ff, cols), lambda step, pos: (0, 0)),
                ]
                + [pl.BlockSpec((NY, PIECE, units), lambda step, pos: (0, 0, 0))] * len(pieces),
                out_specs=pl.BlockSpec((size, NC * cols), lambda step, pos: (0, 0)),
            ),
            out_shape=sds((size, NC * cols), BF16),
            compiler_params=params(24),
            cost_estimate=cost(
                2 * size * ff * NC * cols, 2 * ff * NC * cols + 2 * size * NC * cols
            ),
        )(pos, w_down, others[2], *pieces)
        done.append((blocks, result))
        returned.append(lax.all_to_all(result, ("x", "z"), 0, 0, tiled=True))

    total = None
    last = len(CHUNKS) - 1
    for group in (range(last), range(last, last + 1)):
        keep, give = pl.pallas_call(
            combine_kernel,
            out_shape=(sds((count, cols), F32), sds((count, cols), BF16)),
            in_specs=[SMEM] + [VMEM] * (2 * len(group)),
            out_specs=(VMEM, VMEM),
            compiler_params=params(16),
            cost_estimate=cost(4 * count * cols * 512, 1 << 20),
        )(pos, *[item for i in group for item in (mixes[i], returned[i])])
        give = lax.ppermute(give, "c", [(0, 1), (1, 0)])
        share = keep + give.astype(F32)
        total = share if total is None else total + share
    return total.astype(BF16)


def solution(mesh):
    grid = Mesh(mesh.devices.reshape(NY, NC, NX, NZ), ("y", "c", "x", "z"))
    enc, exp = ("y", "c"), ("x", "z")
    return jax.shard_map(
        body,
        mesh=grid,
        in_specs=(
            P(exp, None),
            P(),
            P(),
            P(exp, None),
            P(exp, enc, None),
            P(exp, enc, None),
            P(exp, None, enc),
        ),
        out_specs=P(exp, enc),
        check_vma=False,
    )
```

```python
import functools

import jax
import jax.numpy as jnp
from jax import lax
from jax.experimental import pallas as pl
from jax.experimental.pallas import tpu as pltpu
from jax.sharding import Mesh, PartitionSpec as P

EPS = 1e-06
F32 = jnp.float32
BF16 = jnp.bfloat16
NY, NC, NX, NZ = 4, 2, 4, 8
N_EXP = NX * NZ
CHUNKS = ((0, 8), (8, 16), (24, 8))
PIECE = 256

VMEM = pl.BlockSpec(memory_space=pltpu.VMEM)
SMEM = pl.BlockSpec(memory_space=pltpu.SMEM)


def by_rows(left, right):
    return lax.dot_general(
        left, right, (((1,), (1,)), ((), ())), preferred_element_type=F32
    )


def times(left, right):
    return jnp.dot(left, right, preferred_element_type=F32)


def params(mib):
    return pltpu.CompilerParams(vmem_limit_bytes=mib << 20)


def cost(flops, moved):
    return pl.CostEstimate(flops=flops, bytes_accessed=moved, transcendentals=0)


def places(names, core):
    tokens = names.shape[1]
    expert = core.astype(F32) + 2.0 * lax.broadcasted_iota(
        jnp.int32, (N_EXP, tokens), 0
    ).astype(F32)
    hits = [names[k : k + 1, :] == expert for k in range(8)]
    named = hits[0]
    for hit in hits[1:]:
        named = named | hit
    row = lax.broadcasted_iota(jnp.int32, (tokens, tokens), 0)
    col = lax.broadcasted_iota(jnp.int32, (tokens, tokens), 1)
    earlier = jnp.where(row < col, 1.0, 0.0).astype(BF16)
    before = times(jnp.where(named, 1.0, 0.0).astype(BF16), earlier)
    return hits, jnp.where(named, before, -1.0)


def spread(place, values, first, size):
    tokens = place.shape[1]
    slot = lax.broadcasted_iota(jnp.int32, (size, tokens), 0) + first
    slot = slot.astype(F32)
    return jnp.concatenate(
        [
            jnp.where(place[d : d + 1, :] == slot, values[d : d + 1, :], 0.0)
            for d in range(N_EXP)
        ],
        axis=0,
    )


def pick(names, part, chunk, core):
    _, place = places(names, core)
    picks = spread(place, jnp.ones_like(place), *chunk).astype(BF16)
    return times(picks, part).astype(BF16)


def first_kernel(pos, tokens, gain, routes, part_out, rows_out):
    values = tokens[...].astype(F32)
    count, width = values.shape
    squares = jnp.sum(values * values, axis=1, keepdims=True)
    inverse = lax.rsqrt(squares / width + EPS)
    quarter = width // NY
    cols = pl.ds(pl.multiple_of(pos[0] * quarter, quarter), quarter)
    mine = (tokens[:, cols].astype(F32) * gain[:, cols].astype(F32)).astype(BF16)
    part = (mine.astype(F32) * inverse).astype(BF16)
    part_out[...] = part
    rows_out[...] = pick(routes[...].astype(F32), part, CHUNKS[0], pos[1])


def later_kernel(pos, part, routes, *rows_out):
    for chunk, out in zip(CHUNKS[1:], rows_out):
        out[...] = pick(routes[...].astype(F32), part[...], chunk, pos[1])


def mix_kernel(pos, tokens, gain, router, routes, *mix_out):
    values = tokens[...].astype(F32)
    count, width = values.shape
    scaled = (values * gain[...].astype(F32)).astype(BF16)
    squares = jnp.sum(values * values, axis=1, keepdims=True)
    inverse = lax.rsqrt(squares / width + EPS)
    turned = jnp.transpose(jnp.broadcast_to(inverse, (count, 128)))
    logits = by_rows(router[...], scaled) * turned[0:1, :]
    expert = lax.broadcasted_iota(jnp.int32, logits.shape, 0).astype(F32)
    names = routes[...].astype(F32)
    chosen = [
        jnp.sum(jnp.where(names[k : k + 1, :] == expert, logits, 0.0), axis=0, keepdims=True)
        for k in range(8)
    ]
    raised = jnp.exp(jnp.concatenate(chosen, axis=0))
    weights = raised / jnp.sum(raised, axis=0, keepdims=True)
    hits, place = places(names, pos[1])
    dense = jnp.zeros_like(place)
    for k in range(8):
        dense = dense + jnp.where(hits[k], weights[k : k + 1, :], 0.0)
    for (first, size), out in zip(CHUNKS, mix_out):
        out[...] = jnp.transpose(spread(place, dense, first, size)).astype(BF16)


def hidden_kernel(pos, blocks, gate_own, gate_other, up_own, up_other, out, *sums):
    step = pl.program_id(0)
    block = blocks[0]
    for total, rows in zip(
        sums, (gate_own[0], up_own[0], gate_other[...], up_other[...])
    ):
        term = by_rows(block, rows)

        @pl.when(step == 0)
        def _(total=total, term=term):
            total[...] = term

        @pl.when(step > 0)
        def _(total=total, term=term):
            total[...] += term

    @pl.when(step == NY - 1)
    def _():
        own, other = [
            gate[...] / (1.0 + jnp.exp(-gate[...])) * up[...]
            for gate, up in (sums[0:2], sums[2:4])
        ]
        low = jnp.where(pos[1] == 0, own, other)
        high = jnp.where(pos[1] == 0, other, own)
        out[...] = jnp.concatenate([low, high], axis=1).astype(BF16)


def store_columns(pos, out, own, other):
    cols = own.shape[1]
    for core, total in ((pos[1], own), (1 - pos[1], other)):
        out[:, pl.ds(pl.multiple_of(core * cols, cols), cols)] = total.astype(BF16)


def down_kernel(pos, blocks, down_own, down_other, out, *sums):
    step = pl.program_id(0)
    for total, part in zip(sums, (down_own[0], down_other[...])):
        term = times(blocks[0], part)

        @pl.when(step == 0)
        def _(total=total, term=term):
            total[...] = term

        @pl.when(step > 0)
        def _(total=total, term=term):
            total[...] += term

    @pl.when(step == NY - 1)
    def _():
        store_columns(pos, out, sums[0][...], sums[1][...])


def down_ring_kernel(pos, down_own, down_other, own, low, high, far_top, far_bottom, out):
    units = own.shape[1]
    far = jnp.concatenate([far_top[...], far_bottom[...]], axis=0)
    mine = theirs = None
    for block, shift in ((own[...], 0), (low[...], 3), (high[...], 1), (far, 2)):
        index = lax.rem(pos[0] + shift, NY)
        rows = pl.ds(pl.multiple_of(index * units, units), units)
        mine_step = times(block, down_own[0, rows, :])
        theirs_step = times(block, down_other[rows, :])
        mine = mine_step if mine is None else mine + mine_step
        theirs = theirs_step if theirs is None else theirs + theirs_step
    store_columns(pos, out, mine, theirs)


def combine_kernel(pos, *refs):
    keep_out, give_out = refs[-2:]
    cols = keep_out.shape[1]
    pairs = len(refs) // 2 - 1
    for out, core in ((give_out, 1 - pos[1]), (keep_out, pos[1])):
        at = pl.ds(pl.multiple_of(core * cols, cols), cols)
        total = None
        for index in range(pairs):
            step = times(refs[2 * index][...], refs[2 * index + 1][:, at])
            total = step if total is None else total + step
        out[...] = total.astype(out.dtype)


def turn(array, step):
    return lax.ppermute(array, "y", [(i, (i + step) % NY) for i in range(NY)])


def ring(block):
    half = block.shape[0] // 2
    low = turn(block, 1)
    high = turn(block, -1)
    return block, low, high, turn(low[:half], 1), turn(high[half:], -1)


def body(tokens, norm_gain, router, routes, w_gate, w_up, w_down):
    count, width = tokens.shape
    quarter = width // NY
    units = 2 * w_gate.shape[1]
    ff = w_down.shape[1]
    cols = w_down.shape[2]
    sds = jax.ShapeDtypeStruct
    pos = jnp.stack([lax.axis_index("y"), lax.axis_index("c")]).astype(jnp.int32)
    turned = routes.T
    sizes = [N_EXP * size for _, size in CHUNKS]

    gain = norm_gain[None, :]
    part, first_rows = pl.pallas_call(
        first_kernel,
        out_shape=(sds((count, quarter), BF16), sds((sizes[0], quarter), BF16)),
        in_specs=[SMEM] + [VMEM] * 3,
        out_specs=(VMEM, VMEM),
        compiler_params=params(16),
        cost_estimate=cost(2 * count * sizes[0] * quarter, count * width * 2),
    )(pos, tokens, gain, turned)
    received = [lax.all_to_all(first_rows, ("x", "z"), 0, 0, tiled=True)]
    later_rows = pl.pallas_call(
        later_kernel,
        out_shape=tuple(sds((size, quarter), BF16) for size in sizes[1:]),
        in_specs=[SMEM] + [VMEM] * 2,
        out_specs=(VMEM,) * (len(CHUNKS) - 1),
        compiler_params=params(16),
        cost_estimate=cost(2 * count * sum(sizes) * quarter, sum(sizes) * quarter * 2),
    )(pos, part, turned)
    sent = [
        lax.dynamic_index_in_dim(array, 1 - pos[1], 0, keepdims=False)
        for array in (w_gate, w_up, w_down)
    ]
    *sent, received[0] = lax.optimization_barrier((*sent, received[0]))
    others = [lax.ppermute(array, "c", [(0, 1), (1, 0)]) for array in sent]
    for rows in later_rows:
        rows, received[-1] = lax.optimization_barrier((rows, received[-1]))
        received.append(lax.all_to_all(rows, ("x", "z"), 0, 0, tiled=True))
    tokens, router, received[0] = lax.optimization_barrier((tokens, router, received[0]))
    mixes = pl.pallas_call(
        mix_kernel,
        out_shape=tuple(sds((count, size), BF16) for size in sizes),
        in_specs=[SMEM] + [VMEM] * 4,
        out_specs=(VMEM,) * len(CHUNKS),
        compiler_params=params(16),
        cost_estimate=cost(2 * count * width * 64, count * width * 2),
    )(pos, tokens, gain, router, turned)

    returned = []
    done = []
    for index, size in enumerate(sizes):
        mine = received[index]
        if index:
            before = [done[i][j] for i, j in ((index - 1, 0), (index - 2, 1)) if i >= 0]
            mine, *before = lax.optimization_barrier((mine, *before))
        blocks = lax.all_gather(mine, "y", axis=0)
        if index == 1:
            blocks, returned[0] = lax.optimization_barrier((blocks, returned[0]))
        own_weight = pl.BlockSpec((1, units // 2, quarter), lambda y, pos: (pos[1], 0, y))
        other_weight = pl.BlockSpec((units // 2, quarter), lambda y, pos: (0, y))
        hidden = pl.pallas_call(
            hidden_kernel,
            grid_spec=pltpu.PrefetchScalarGridSpec(
                num_scalar_prefetch=1,
                grid=(NY,),
                in_specs=[
                    pl.BlockSpec((1, size, quarter), lambda y, pos: (y, 0, 0)),
                    own_weight,
                    other_weight,
                    own_weight,
                    other_weight,
                ],
                out_specs=pl.BlockSpec((size, units), lambda y, pos: (0, 0)),
                scratch_shapes=[pltpu.VMEM((size, units // 2), F32)] * 4,
            ),
            out_shape=sds((size, units), BF16),
            compiler_params=params(56),
            cost_estimate=cost(4 * size * width * units, 4 * units * width + 2 * size * width),
        )(pos, blocks, w_gate, others[0], w_up, others[1])
        down_cost = cost(
            2 * size * ff * NC * cols, 2 * ff * NC * cols + 2 * size * NC * cols
        )
        if size > PIECE:
            whole = pl.BlockSpec((size, units), lambda step, pos: (0, 0))
            half = pl.BlockSpec((size // 2, units), lambda step, pos: (0, 0))
            result = pl.pallas_call(
                down_ring_kernel,
                grid_spec=pltpu.PrefetchScalarGridSpec(
                    num_scalar_prefetch=1,
                    grid=(1,),
                    in_specs=[
                        pl.BlockSpec((1, ff, cols), lambda step, pos: (pos[1], 0, 0)),
                        pl.BlockSpec((ff, cols), lambda step, pos: (0, 0)),
                        whole,
                        whole,
                        whole,
                        half,
                        half,
                    ],
                    out_specs=pl.BlockSpec((size, NC * cols), lambda step, pos: (0, 0)),
                ),
                out_shape=sds((size, NC * cols), BF16),
                compiler_params=params(56),
                cost_estimate=down_cost,
            )(pos, w_down, others[2], *ring(hidden))
        else:
            result = pl.pallas_call(
                down_kernel,
                grid_spec=pltpu.PrefetchScalarGridSpec(
                    num_scalar_prefetch=1,
                    grid=(NY,),
                    in_specs=[
                        pl.BlockSpec((1, size, units), lambda y, pos: (y, 0, 0)),
                        pl.BlockSpec((1, units, cols), lambda y, pos: (pos[1], y, 0)),
                        pl.BlockSpec((units, cols), lambda y, pos: (y, 0)),
                    ],
                    out_specs=pl.BlockSpec((size, NC * cols), lambda y, pos: (0, 0)),
                    scratch_shapes=[pltpu.VMEM((size, cols), F32)] * 2,
                ),
                out_shape=sds((size, NC * cols), BF16),
                compiler_params=params(56),
                cost_estimate=down_cost,
            )(pos, lax.all_gather(hidden, "y", axis=0), w_down, others[2])
        if index == 0:
            result, received[-1] = lax.optimization_barrier((result, received[-1]))
        done.append((blocks, result))
        returned.append(lax.all_to_all(result, ("x", "z"), 0, 0, tiled=True))

    total = None
    last = len(CHUNKS) - 1
    for group in (range(last), range(last, last + 1)):
        keep, give = pl.pallas_call(
            combine_kernel,
            out_shape=(sds((count, cols), F32), sds((count, cols), BF16)),
            in_specs=[SMEM] + [VMEM] * (2 * len(group)),
            out_specs=(VMEM, VMEM),
            compiler_params=params(16),
            cost_estimate=cost(4 * count * cols * 512, 1 << 20),
        )(pos, *[item for i in group for item in (mixes[i], returned[i])])
        give = lax.ppermute(give, "c", [(0, 1), (1, 0)])
        share = keep + give.astype(F32)
        total = share if total is None else total + share
    return total.astype(BF16)


def solution(mesh):
    grid = Mesh(mesh.devices.reshape(NY, NC, NX, NZ), ("y", "c", "x", "z"))
    enc, exp = ("y", "c"), ("x", "z")
    return jax.shard_map(
        body,
        mesh=grid,
        in_specs=(
            P(exp, None),
            P(),
            P(),
            P(exp, None),
            P(exp, enc, None),
            P(exp, enc, None),
            P(exp, None, enc),
        ),
        out_specs=P(exp, enc),
        check_vma=False,
    )
```

```python
import functools

import jax
import jax.numpy as jnp
from jax import lax
from jax.experimental import pallas as pl
from jax.experimental.pallas import tpu as pltpu
from jax.sharding import Mesh, PartitionSpec as P

EPS = 1e-06
F32 = jnp.float32
BF16 = jnp.bfloat16
NY, NC, NX, NZ = 4, 2, 4, 8
N_EXP = NX * NZ
CHUNKS = ((0, 8), (8, 16), (24, 8))
PIECE = 256

VMEM = pl.BlockSpec(memory_space=pltpu.VMEM)
SMEM = pl.BlockSpec(memory_space=pltpu.SMEM)


def by_rows(left, right):
    return lax.dot_general(
        left, right, (((1,), (1,)), ((), ())), preferred_element_type=F32
    )


def times(left, right):
    return jnp.dot(left, right, preferred_element_type=F32)


def params(mib):
    return pltpu.CompilerParams(vmem_limit_bytes=mib << 20)


def cost(flops, moved):
    return pl.CostEstimate(flops=flops, bytes_accessed=moved, transcendentals=0)


def places(names, core):
    tokens = names.shape[1]
    expert = core.astype(F32) + 2.0 * lax.broadcasted_iota(
        jnp.int32, (N_EXP, tokens), 0
    ).astype(F32)
    hits = [names[k : k + 1, :] == expert for k in range(8)]
    named = hits[0]
    for hit in hits[1:]:
        named = named | hit
    row = lax.broadcasted_iota(jnp.int32, (tokens, tokens), 0)
    col = lax.broadcasted_iota(jnp.int32, (tokens, tokens), 1)
    earlier = jnp.where(row < col, 1.0, 0.0).astype(BF16)
    before = times(jnp.where(named, 1.0, 0.0).astype(BF16), earlier)
    return hits, jnp.where(named, before, -1.0)


def spread(place, values, first, size):
    tokens = place.shape[1]
    slot = lax.broadcasted_iota(jnp.int32, (size, tokens), 0) + first
    slot = slot.astype(F32)
    return jnp.concatenate(
        [
            jnp.where(place[d : d + 1, :] == slot, values[d : d + 1, :], 0.0)
            for d in range(N_EXP)
        ],
        axis=0,
    )


def pick(names, part, chunk, core):
    _, place = places(names, core)
    picks = spread(place, jnp.ones_like(place), *chunk).astype(BF16)
    return times(picks, part).astype(BF16)


def first_kernel(pos, tokens, gain, routes, part_out, rows_out):
    values = tokens[...].astype(F32)
    count, width = values.shape
    squares = jnp.sum(values * values, axis=1, keepdims=True)
    inverse = lax.rsqrt(squares / width + EPS)
    quarter = width // NY
    cols = pl.ds(pl.multiple_of(pos[0] * quarter, quarter), quarter)
    mine = (tokens[:, cols].astype(F32) * gain[:, cols].astype(F32)).astype(BF16)
    part = (mine.astype(F32) * inverse).astype(BF16)
    part_out[...] = part
    rows_out[...] = pick(routes[...].astype(F32), part, CHUNKS[0], pos[1])


def later_kernel(pos, part, routes, *rows_out):
    for chunk, out in zip(CHUNKS[1:], rows_out):
        out[...] = pick(routes[...].astype(F32), part[...], chunk, pos[1])


def mix_kernel(pos, tokens, gain, router, routes, *mix_out):
    values = tokens[...].astype(F32)
    count, width = values.shape
    scaled = (values * gain[...].astype(F32)).astype(BF16)
    squares = jnp.sum(values * values, axis=1, keepdims=True)
    inverse = lax.rsqrt(squares / width + EPS)
    turned = jnp.transpose(jnp.broadcast_to(inverse, (count, 128)))
    logits = by_rows(router[...], scaled) * turned[0:1, :]
    expert = lax.broadcasted_iota(jnp.int32, logits.shape, 0).astype(F32)
    names = routes[...].astype(F32)
    chosen = [
        jnp.sum(jnp.where(names[k : k + 1, :] == expert, logits, 0.0), axis=0, keepdims=True)
        for k in range(8)
    ]
    raised = jnp.exp(jnp.concatenate(chosen, axis=0))
    weights = raised / jnp.sum(raised, axis=0, keepdims=True)
    hits, place = places(names, pos[1])
    dense = jnp.zeros_like(place)
    for k in range(8):
        dense = dense + jnp.where(hits[k], weights[k : k + 1, :], 0.0)
    for (first, size), out in zip(CHUNKS, mix_out):
        out[...] = jnp.transpose(spread(place, dense, first, size)).astype(BF16)


def hidden_kernel(pos, blocks, gate_own, gate_other, up_own, up_other, out):
    quarter = blocks.shape[2]
    sums = [None] * 4
    for y in range(NY):
        block = blocks[y]
        cols = slice(y * quarter, (y + 1) * quarter)
        for which, weight in enumerate((gate_own, up_own, gate_other, up_other)):
            term = by_rows(weight[:, cols], block)
            sums[which] = term if y == 0 else sums[which] + term
    own, other = [
        gate / (1.0 + jnp.exp(-gate)) * up for gate, up in (sums[0:2], sums[2:4])
    ]
    low = jnp.where(pos[1] == 0, own, other)
    high = jnp.where(pos[1] == 0, other, own)
    out[...] = jnp.transpose(jnp.concatenate([low, high], axis=0)).astype(BF16)


def down_kernel(pos, down_own, down_other, *refs):
    out = refs[-1]
    cols = down_other.shape[1]
    for index, blocks in enumerate(refs[:-1]):
        rows, units = blocks.shape[1:]
        at = slice(index * rows, (index + 1) * rows)
        own = other = None
        for y in range(NY):
            span = slice(y * units, (y + 1) * units)
            own_term = times(blocks[y], down_own[span, :])
            other_term = times(blocks[y], down_other[span, :])
            own = own_term if y == 0 else own + own_term
            other = other_term if y == 0 else other + other_term
        for core, total in ((pos[1], own), (1 - pos[1], other)):
            out[at, pl.ds(pl.multiple_of(core * cols, cols), cols)] = total.astype(BF16)


def combine_kernel(pos, *refs):
    keep_out, give_out = refs[-2:]
    cols = keep_out.shape[1]
    pairs = len(refs) // 2 - 1
    for out, core in ((give_out, 1 - pos[1]), (keep_out, pos[1])):
        at = pl.ds(pl.multiple_of(core * cols, cols), cols)
        total = None
        for index in range(pairs):
            step = times(refs[2 * index][...], refs[2 * index + 1][:, at])
            total = step if total is None else total + step
        out[...] = total.astype(out.dtype)


def body(tokens, norm_gain, router, routes, w_gate, w_up, w_down):
    count, width = tokens.shape
    quarter = width // NY
    units = 2 * w_gate.shape[1]
    ff = w_down.shape[1]
    cols = w_down.shape[2]
    sds = jax.ShapeDtypeStruct
    pos = jnp.stack([lax.axis_index("y"), lax.axis_index("c")]).astype(jnp.int32)
    turned = routes.T
    sizes = [N_EXP * size for _, size in CHUNKS]

    gain = norm_gain[None, :]
    part, first_rows = pl.pallas_call(
        first_kernel,
        out_shape=(sds((count, quarter), BF16), sds((sizes[0], quarter), BF16)),
        in_specs=[SMEM] + [VMEM] * 3,
        out_specs=(VMEM, VMEM),
        compiler_params=params(16),
        cost_estimate=cost(2 * count * sizes[0] * quarter, count * width * 2),
    )(pos, tokens, gain, turned)
    received = [lax.all_to_all(first_rows, ("x", "z"), 0, 0, tiled=True)]
    later_rows = pl.pallas_call(
        later_kernel,
        out_shape=tuple(sds((size, quarter), BF16) for size in sizes[1:]),
        in_specs=[SMEM] + [VMEM] * 2,
        out_specs=(VMEM,) * (len(CHUNKS) - 1),
        compiler_params=params(16),
        cost_estimate=cost(2 * count * sum(sizes) * quarter, sum(sizes) * quarter * 2),
    )(pos, part, turned)
    arrays = (w_gate, w_up, w_down)
    sent, own = [
        [lax.dynamic_index_in_dim(array, core, 0, keepdims=False) for array in arrays]
        for core in (1 - pos[1], pos[1])
    ]
    *sent, received[0] = lax.optimization_barrier((*sent, received[0]))
    *own, received[0] = lax.optimization_barrier((*own, received[0]))
    others = [lax.ppermute(array, "c", [(0, 1), (1, 0)]) for array in sent]
    for rows in later_rows:
        rows, received[-1] = lax.optimization_barrier((rows, received[-1]))
        received.append(lax.all_to_all(rows, ("x", "z"), 0, 0, tiled=True))
    tokens, router, received[0] = lax.optimization_barrier((tokens, router, received[0]))
    mixes = pl.pallas_call(
        mix_kernel,
        out_shape=tuple(sds((count, size), BF16) for size in sizes),
        in_specs=[SMEM] + [VMEM] * 4,
        out_specs=(VMEM,) * len(CHUNKS),
        compiler_params=params(16),
        cost_estimate=cost(2 * count * width * 64, count * width * 2),
    )(pos, tokens, gain, router, turned)

    returned = []
    done = []
    for index, size in enumerate(sizes):
        mine = received[index]
        if index:
            before = [done[i][j] for i, j in ((index - 1, 0), (index - 2, 1)) if i >= 0]
            mine, *before = lax.optimization_barrier((mine, *before))
        blocks = lax.all_gather(mine, "y", axis=0)
        if index == 1:
            blocks, returned[0] = lax.optimization_barrier((blocks, returned[0]))
        pieces = []
        for half in range(size // PIECE):
            hidden = pl.pallas_call(
                hidden_kernel,
                grid_spec=pltpu.PrefetchScalarGridSpec(
                    num_scalar_prefetch=1,
                    grid=(1,),
                    in_specs=[
                        pl.BlockSpec(
                            (NY, PIECE, quarter), lambda step, pos, half=half: (0, half, 0)
                        )
                    ]
                    + [pl.BlockSpec((units // 2, width), lambda step, pos: (0, 0))] * 4,
                    out_specs=pl.BlockSpec((PIECE, units), lambda step, pos: (0, 0)),
                ),
                out_shape=sds((PIECE, units), BF16),
                compiler_params=params(24),
                cost_estimate=cost(
                    4 * PIECE * width * units, 4 * units * width + 2 * PIECE * width
                ),
            )(pos, blocks, own[0], others[0], own[1], others[1])
            pieces.append(lax.all_gather(hidden, "y", axis=0))
        result = pl.pallas_call(
            down_kernel,
            grid_spec=pltpu.PrefetchScalarGridSpec(
                num_scalar_prefetch=1,
                grid=(1,),
                in_specs=[pl.BlockSpec((ff, cols), lambda step, pos: (0, 0))] * 2
                + [pl.BlockSpec((NY, PIECE, units), lambda step, pos: (0, 0, 0))] * len(pieces),
                out_specs=pl.BlockSpec((size, NC * cols), lambda step, pos: (0, 0)),
            ),
            out_shape=sds((size, NC * cols), BF16),
            compiler_params=params(24),
            cost_estimate=cost(
                2 * size * ff * NC * cols, 2 * ff * NC * cols + 2 * size * NC * cols
            ),
        )(pos, own[2], others[2], *pieces)
        if index == 0:
            result, received[-1] = lax.optimization_barrier((result, received[-1]))
        done.append((blocks, result))
        returned.append(lax.all_to_all(result, ("x", "z"), 0, 0, tiled=True))

    total = None
    last = len(CHUNKS) - 1
    for group in (range(last), range(last, last + 1)):
        keep, give = pl.pallas_call(
            combine_kernel,
            out_shape=(sds((count, cols), F32), sds((count, cols), BF16)),
            in_specs=[SMEM] + [VMEM] * (2 * len(group)),
            out_specs=(VMEM, VMEM),
            compiler_params=params(16),
            cost_estimate=cost(4 * count * cols * 512, 1 << 20),
        )(pos, *[item for i in group for item in (mixes[i], returned[i])])
        give = lax.ppermute(give, "c", [(0, 1), (1, 0)])
        share = keep + give.astype(F32)
        total = share if total is None else total + share
    return total.astype(BF16)


def solution(mesh):
    grid = Mesh(mesh.devices.reshape(NY, NC, NX, NZ), ("y", "c", "x", "z"))
    enc, exp = ("y", "c"), ("x", "z")
    return jax.shard_map(
        body,
        mesh=grid,
        in_specs=(
            P(exp, None),
            P(),
            P(),
            P(exp, None),
            P(exp, enc, None),
            P(exp, enc, None),
            P(exp, None, enc),
        ),
        out_specs=P(exp, enc),
        check_vma=False,
    )
```

```python
import functools

import jax
import jax.numpy as jnp
from jax import lax
from jax.experimental import pallas as pl
from jax.experimental.pallas import tpu as pltpu
from jax.sharding import Mesh, PartitionSpec as P

EPS = 1e-06
F32 = jnp.float32
BF16 = jnp.bfloat16
NY, NC, NX, NZ = 4, 2, 4, 8
N_EXP = NX * NZ
CHUNKS = ((0, 8), (8, 16), (24, 8))
PIECE = 256

VMEM = pl.BlockSpec(memory_space=pltpu.VMEM)
SMEM = pl.BlockSpec(memory_space=pltpu.SMEM)


def by_rows(left, right):
    return lax.dot_general(
        left, right, (((1,), (1,)), ((), ())), preferred_element_type=F32
    )


def times(left, right):
    return jnp.dot(left, right, preferred_element_type=F32)


def params(mib):
    return pltpu.CompilerParams(vmem_limit_bytes=mib << 20)


def cost(flops, moved):
    return pl.CostEstimate(flops=flops, bytes_accessed=moved, transcendentals=0)


def places(names, core):
    tokens = names.shape[1]
    expert = core.astype(F32) + 2.0 * lax.broadcasted_iota(
        jnp.int32, (N_EXP, tokens), 0
    ).astype(F32)
    hits = [names[k : k + 1, :] == expert for k in range(8)]
    named = hits[0]
    for hit in hits[1:]:
        named = named | hit
    row = lax.broadcasted_iota(jnp.int32, (tokens, tokens), 0)
    col = lax.broadcasted_iota(jnp.int32, (tokens, tokens), 1)
    earlier = jnp.where(row < col, 1.0, 0.0).astype(BF16)
    before = times(jnp.where(named, 1.0, 0.0).astype(BF16), earlier)
    return hits, jnp.where(named, before, -1.0)


def spread(place, values, first, size):
    tokens = place.shape[1]
    slot = lax.broadcasted_iota(jnp.int32, (size, tokens), 0) + first
    slot = slot.astype(F32)
    return jnp.concatenate(
        [
            jnp.where(place[d : d + 1, :] == slot, values[d : d + 1, :], 0.0)
            for d in range(N_EXP)
        ],
        axis=0,
    )


def pick(names, part, chunk, core):
    _, place = places(names, core)
    picks = spread(place, jnp.ones_like(place), *chunk).astype(BF16)
    return times(picks, part).astype(BF16)


def first_kernel(pos, tokens, gain, routes, part_out, rows_out):
    values = tokens[...].astype(F32)
    count, width = values.shape
    squares = jnp.sum(values * values, axis=1, keepdims=True)
    inverse = lax.rsqrt(squares / width + EPS)
    quarter = width // NY
    cols = pl.ds(pl.multiple_of(pos[0] * quarter, quarter), quarter)
    mine = (tokens[:, cols].astype(F32) * gain[:, cols].astype(F32)).astype(BF16)
    part = (mine.astype(F32) * inverse).astype(BF16)
    part_out[...] = part
    rows_out[...] = pick(routes[...].astype(F32), part, CHUNKS[0], pos[1])


def later_kernel(pos, part, routes, *rows_out):
    for chunk, out in zip(CHUNKS[1:], rows_out):
        out[...] = pick(routes[...].astype(F32), part[...], chunk, pos[1])


def mix_kernel(pos, tokens, gain, router, routes, *mix_out):
    values = tokens[...].astype(F32)
    count, width = values.shape
    scaled = (values * gain[...].astype(F32)).astype(BF16)
    squares = jnp.sum(values * values, axis=1, keepdims=True)
    inverse = lax.rsqrt(squares / width + EPS)
    turned = jnp.transpose(jnp.broadcast_to(inverse, (count, 128)))
    logits = by_rows(router[...], scaled) * turned[0:1, :]
    expert = lax.broadcasted_iota(jnp.int32, logits.shape, 0).astype(F32)
    names = routes[...].astype(F32)
    chosen = [
        jnp.sum(jnp.where(names[k : k + 1, :] == expert, logits, 0.0), axis=0, keepdims=True)
        for k in range(8)
    ]
    raised = jnp.exp(jnp.concatenate(chosen, axis=0))
    weights = raised / jnp.sum(raised, axis=0, keepdims=True)
    hits, place = places(names, pos[1])
    dense = jnp.zeros_like(place)
    for k in range(8):
        dense = dense + jnp.where(hits[k], weights[k : k + 1, :], 0.0)
    for (first, size), out in zip(CHUNKS, mix_out):
        out[...] = jnp.transpose(spread(place, dense, first, size)).astype(BF16)


def hidden_kernel(half, pos, blocks, gate_own, gate_other, up_own, up_other, out):
    quarter = blocks.shape[2]
    rows = slice(half * PIECE, (half + 1) * PIECE)
    sums = [None] * 4
    for y in range(NY):
        block = blocks[y, rows, :]
        cols = slice(y * quarter, (y + 1) * quarter)
        for which, weight in enumerate((gate_own, up_own, gate_other, up_other)):
            term = by_rows(weight[:, cols], block)
            sums[which] = term if y == 0 else sums[which] + term
    own, other = [
        gate / (1.0 + jnp.exp(-gate)) * up for gate, up in (sums[0:2], sums[2:4])
    ]
    low = jnp.where(pos[1] == 0, own, other)
    high = jnp.where(pos[1] == 0, other, own)
    out[...] = jnp.transpose(jnp.concatenate([low, high], axis=0)).astype(BF16)


def store_columns(pos, out, at, own, other):
    cols = own.shape[1]
    for core, total in ((pos[1], own), (1 - pos[1], other)):
        out[at, pl.ds(pl.multiple_of(core * cols, cols), cols)] = total.astype(BF16)


def down_kernel(pos, down_own, down_other, blocks, out):
    rows, units = blocks.shape[1:]
    own = other = None
    for y in range(NY):
        span = slice(y * units, (y + 1) * units)
        own_term = times(blocks[y], down_own[span, :])
        other_term = times(blocks[y], down_other[span, :])
        own = own_term if y == 0 else own + own_term
        other = other_term if y == 0 else other + other_term
    store_columns(pos, out, slice(0, rows), own, other)


def down_ring_kernel(pos, down_own, down_other, *refs):
    out = refs[-1]
    for index in range(len(refs) // 5):
        own, low, high, far_top, far_bottom = refs[5 * index : 5 * index + 5]
        rows, units = own.shape
        far = jnp.concatenate([far_top[...], far_bottom[...]], axis=0)
        mine = theirs = None
        for block, step in ((own[...], 0), (low[...], 3), (high[...], 1), (far, 2)):
            at = lax.rem(pos[0] + step, NY)
            span = pl.ds(pl.multiple_of(at * units, units), units)
            own_term = times(block, down_own[span, :])
            other_term = times(block, down_other[span, :])
            mine = own_term if mine is None else mine + own_term
            theirs = other_term if theirs is None else theirs + other_term
        store_columns(pos, out, slice(index * rows, (index + 1) * rows), mine, theirs)


def combine_kernel(pos, *refs):
    keep_out, give_out = refs[-2:]
    cols = keep_out.shape[1]
    pairs = len(refs) // 2 - 1
    for out, core in ((give_out, 1 - pos[1]), (keep_out, pos[1])):
        at = pl.ds(pl.multiple_of(core * cols, cols), cols)
        total = None
        for index in range(pairs):
            step = times(refs[2 * index][...], refs[2 * index + 1][:, at])
            total = step if total is None else total + step
        out[...] = total.astype(out.dtype)


def turn(array, step):
    return lax.ppermute(array, "y", [(i, (i + step) % NY) for i in range(NY)])


def ring(block):
    half = block.shape[0] // 2
    low = turn(block, 1)
    high = turn(block, -1)
    return block, low, high, turn(low[:half], 1), turn(high[half:], -1)


def body(tokens, norm_gain, router, routes, w_gate, w_up, w_down):
    count, width = tokens.shape
    quarter = width // NY
    units = 2 * w_gate.shape[1]
    ff = w_down.shape[1]
    cols = w_down.shape[2]
    sds = jax.ShapeDtypeStruct
    pos = jnp.stack([lax.axis_index("y"), lax.axis_index("c")]).astype(jnp.int32)
    turned = routes.T
    sizes = [N_EXP * size for _, size in CHUNKS]

    gain = norm_gain[None, :]
    part, first_rows = pl.pallas_call(
        first_kernel,
        out_shape=(sds((count, quarter), BF16), sds((sizes[0], quarter), BF16)),
        in_specs=[SMEM] + [VMEM] * 3,
        out_specs=(VMEM, VMEM),
        compiler_params=params(16),
        cost_estimate=cost(2 * count * sizes[0] * quarter, count * width * 2),
    )(pos, tokens, gain, turned)
    received = [lax.all_to_all(first_rows, ("x", "z"), 0, 0, tiled=True)]
    later_rows = pl.pallas_call(
        later_kernel,
        out_shape=tuple(sds((size, quarter), BF16) for size in sizes[1:]),
        in_specs=[SMEM] + [VMEM] * 2,
        out_specs=(VMEM,) * (len(CHUNKS) - 1),
        compiler_params=params(16),
        cost_estimate=cost(2 * count * sum(sizes) * quarter, sum(sizes) * quarter * 2),
    )(pos, part, turned)
    arrays = (w_gate, w_up, w_down)
    sent, own = [
        [lax.dynamic_index_in_dim(array, core, 0, keepdims=False) for array in arrays]
        for core in (1 - pos[1], pos[1])
    ]
    *sent, received[0] = lax.optimization_barrier((*sent, received[0]))
    *own, received[0] = lax.optimization_barrier((*own, received[0]))
    others = [lax.ppermute(array, "c", [(0, 1), (1, 0)]) for array in sent]
    for rows in later_rows:
        rows, received[-1] = lax.optimization_barrier((rows, received[-1]))
        received.append(lax.all_to_all(rows, ("x", "z"), 0, 0, tiled=True))
    tokens, router, received[0] = lax.optimization_barrier((tokens, router, received[0]))
    mixes = pl.pallas_call(
        mix_kernel,
        out_shape=tuple(sds((count, size), BF16) for size in sizes),
        in_specs=[SMEM] + [VMEM] * 4,
        out_specs=(VMEM,) * len(CHUNKS),
        compiler_params=params(16),
        cost_estimate=cost(2 * count * width * 64, count * width * 2),
    )(pos, tokens, gain, router, turned)

    returned = []
    done = []
    for index, size in enumerate(sizes):
        mine = received[index]
        if index:
            before = [done[i][j] for i, j in ((index - 1, 0), (index - 2, 1)) if i >= 0]
            mine, *before = lax.optimization_barrier((mine, *before))
        blocks = lax.all_gather(mine, "y", axis=0)
        if index == 1:
            blocks, returned[0] = lax.optimization_barrier((blocks, returned[0]))
        pieces = []
        for half in range(size // PIECE):
            hidden = pl.pallas_call(
                functools.partial(hidden_kernel, half),
                out_shape=sds((PIECE, units), BF16),
                in_specs=[SMEM] + [VMEM] * 5,
                out_specs=VMEM,
                compiler_params=params(24),
                cost_estimate=cost(
                    4 * PIECE * width * units, 4 * units * width + 2 * PIECE * width
                ),
            )(pos, blocks, own[0], others[0], own[1], others[1])
            if size > PIECE:
                pieces.extend(ring(hidden))
            else:
                pieces.append(lax.all_gather(hidden, "y", axis=0))
        result = pl.pallas_call(
            down_ring_kernel if size > PIECE else down_kernel,
            out_shape=sds((size, NC * cols), BF16),
            in_specs=[SMEM] + [VMEM] * (2 + len(pieces)),
            out_specs=VMEM,
            compiler_params=params(24),
            cost_estimate=cost(
                2 * size * ff * NC * cols, 2 * ff * NC * cols + 2 * size * NC * cols
            ),
        )(pos, own[2], others[2], *pieces)
        if index == 0:
            result, received[-1] = lax.optimization_barrier((result, received[-1]))
        done.append((blocks, result))
        returned.append(lax.all_to_all(result, ("x", "z"), 0, 0, tiled=True))

    total = None
    last = len(CHUNKS) - 1
    for group in (range(last), range(last, last + 1)):
        keep, give = pl.pallas_call(
            combine_kernel,
            out_shape=(sds((count, cols), F32), sds((count, cols), BF16)),
            in_specs=[SMEM] + [VMEM] * (2 * len(group)),
            out_specs=(VMEM, VMEM),
            compiler_params=params(16),
            cost_estimate=cost(4 * count * cols * 512, 1 << 20),
        )(pos, *[item for i in group for item in (mixes[i], returned[i])])
        give = lax.ppermute(give, "c", [(0, 1), (1, 0)])
        share = keep + give.astype(F32)
        total = share if total is None else total + share
    return total.astype(BF16)


def solution(mesh):
    grid = Mesh(mesh.devices.reshape(NY, NC, NX, NZ), ("y", "c", "x", "z"))
    enc, exp = ("y", "c"), ("x", "z")
    return jax.shard_map(
        body,
        mesh=grid,
        in_specs=(
            P(exp, None),
            P(),
            P(),
            P(exp, None),
            P(exp, enc, None),
            P(exp, enc, None),
            P(exp, None, enc),
        ),
        out_specs=P(exp, enc),
        check_vma=False,
    )
```

```python
import functools

import jax
import jax.numpy as jnp
from jax import lax
from jax.experimental import pallas as pl
from jax.experimental.pallas import tpu as pltpu
from jax.sharding import Mesh, PartitionSpec as P

EPS = 1e-06
F32 = jnp.float32
BF16 = jnp.bfloat16
NY, NC, NX, NZ = 4, 2, 4, 8
N_EXP = NX * NZ
CHUNKS = ((0, 8), (8, 16), (24, 8))
PIECE = 256

VMEM = pl.BlockSpec(memory_space=pltpu.VMEM)
SMEM = pl.BlockSpec(memory_space=pltpu.SMEM)


def by_rows(left, right):
    return lax.dot_general(
        left, right, (((1,), (1,)), ((), ())), preferred_element_type=F32
    )


def times(left, right):
    return jnp.dot(left, right, preferred_element_type=F32)


def params(mib):
    return pltpu.CompilerParams(vmem_limit_bytes=mib << 20)


def cost(flops, moved):
    return pl.CostEstimate(flops=flops, bytes_accessed=moved, transcendentals=0)


def places(names, core):
    tokens = names.shape[1]
    expert = core.astype(F32) + 2.0 * lax.broadcasted_iota(
        jnp.int32, (N_EXP, tokens), 0
    ).astype(F32)
    hits = [names[k : k + 1, :] == expert for k in range(8)]
    named = hits[0]
    for hit in hits[1:]:
        named = named | hit
    row = lax.broadcasted_iota(jnp.int32, (tokens, tokens), 0)
    col = lax.broadcasted_iota(jnp.int32, (tokens, tokens), 1)
    earlier = jnp.where(row < col, 1.0, 0.0).astype(BF16)
    before = times(jnp.where(named, 1.0, 0.0).astype(BF16), earlier)
    return hits, jnp.where(named, before, -1.0)


def spread(place, values, first, size):
    tokens = place.shape[1]
    slot = lax.broadcasted_iota(jnp.int32, (size, tokens), 0) + first
    slot = slot.astype(F32)
    return jnp.concatenate(
        [
            jnp.where(place[d : d + 1, :] == slot, values[d : d + 1, :], 0.0)
            for d in range(N_EXP)
        ],
        axis=0,
    )


def pick(names, part, chunk, core):
    _, place = places(names, core)
    picks = spread(place, jnp.ones_like(place), *chunk).astype(BF16)
    return times(picks, part).astype(BF16)


def first_kernel(pos, tokens, gain, routes, part_out, rows_out):
    values = tokens[...].astype(F32)
    count, width = values.shape
    squares = jnp.sum(values * values, axis=1, keepdims=True)
    inverse = lax.rsqrt(squares / width + EPS)
    quarter = width // NY
    cols = pl.ds(pl.multiple_of(pos[0] * quarter, quarter), quarter)
    mine = (tokens[:, cols].astype(F32) * gain[:, cols].astype(F32)).astype(BF16)
    part = (mine.astype(F32) * inverse).astype(BF16)
    part_out[...] = part
    rows_out[...] = pick(routes[...].astype(F32), part, CHUNKS[0], pos[1])


def later_kernel(pos, part, routes, *rows_out):
    for chunk, out in zip(CHUNKS[1:], rows_out):
        out[...] = pick(routes[...].astype(F32), part[...], chunk, pos[1])


def mix_kernel(pos, tokens, gain, router, routes, *mix_out):
    values = tokens[...].astype(F32)
    count, width = values.shape
    scaled = (values * gain[...].astype(F32)).astype(BF16)
    squares = jnp.sum(values * values, axis=1, keepdims=True)
    inverse = lax.rsqrt(squares / width + EPS)
    turned = jnp.transpose(jnp.broadcast_to(inverse, (count, 128)))
    logits = by_rows(router[...], scaled) * turned[0:1, :]
    expert = lax.broadcasted_iota(jnp.int32, logits.shape, 0).astype(F32)
    names = routes[...].astype(F32)
    chosen = [
        jnp.sum(jnp.where(names[k : k + 1, :] == expert, logits, 0.0), axis=0, keepdims=True)
        for k in range(8)
    ]
    raised = jnp.exp(jnp.concatenate(chosen, axis=0))
    weights = raised / jnp.sum(raised, axis=0, keepdims=True)
    hits, place = places(names, pos[1])
    dense = jnp.zeros_like(place)
    for k in range(8):
        dense = dense + jnp.where(hits[k], weights[k : k + 1, :], 0.0)
    for (first, size), out in zip(CHUNKS, mix_out):
        out[...] = jnp.transpose(spread(place, dense, first, size)).astype(BF16)


def activate(pos, sums):
    units = sums.shape[0] // 4
    gate_own, up_own, gate_other, up_other = [
        sums[index * units : (index + 1) * units] for index in range(4)
    ]
    own = gate_own / (1.0 + jnp.exp(-gate_own)) * up_own
    other = gate_other / (1.0 + jnp.exp(-gate_other)) * up_other
    low = jnp.where(pos[1] == 0, own, other)
    high = jnp.where(pos[1] == 0, other, own)
    return jnp.transpose(jnp.concatenate([low, high], axis=0)).astype(BF16)


def hidden_kernel(half, pos, blocks, gate_own, gate_other, up_own, up_other, out):
    quarter = blocks.shape[2]
    rows = slice(half * PIECE, (half + 1) * PIECE)
    total = None
    for y in range(NY):
        cols = slice(y * quarter, (y + 1) * quarter)
        weights = jnp.concatenate(
            [weight[:, cols] for weight in (gate_own, up_own, gate_other, up_other)], axis=0
        )
        term = by_rows(weights, blocks[y, rows, :])
        total = term if y == 0 else total + term
    out[...] = activate(pos, total)


def hidden_ring_kernel(
    pos, own, low, high, far_top, far_bottom, gate_own, gate_other, up_own, up_other, out
):
    quarter = own.shape[1]
    far = jnp.concatenate([far_top[...], far_bottom[...]], axis=0)
    total = None
    for block, step in ((own[...], 0), (low[...], 3), (high[...], 1), (far, 2)):
        at = lax.rem(pos[0] + step, NY)
        cols = pl.ds(pl.multiple_of(at * quarter, quarter), quarter)
        weights = jnp.concatenate(
            [weight[:, cols] for weight in (gate_own, up_own, gate_other, up_other)], axis=0
        )
        term = by_rows(weights, block)
        total = term if total is None else total + term
    out[...] = activate(pos, total)


def store_columns(pos, out, at, own, other):
    cols = own.shape[1]
    for core, total in ((pos[1], own), (1 - pos[1], other)):
        out[at, pl.ds(pl.multiple_of(core * cols, cols), cols)] = total.astype(BF16)


def down_kernel(pos, down_own, down_other, blocks, out):
    rows, units = blocks.shape[1:]
    own = other = None
    for y in range(NY):
        span = slice(y * units, (y + 1) * units)
        own_term = times(blocks[y], down_own[span, :])
        other_term = times(blocks[y], down_other[span, :])
        own = own_term if y == 0 else own + own_term
        other = other_term if y == 0 else other + other_term
    store_columns(pos, out, slice(0, rows), own, other)


def down_ring_kernel(pos, down_own, down_other, *refs):
    out = refs[-1]
    for index in range(len(refs) // 5):
        own, low, high, far_top, far_bottom = refs[5 * index : 5 * index + 5]
        rows, units = own.shape
        far = jnp.concatenate([far_top[...], far_bottom[...]], axis=0)
        mine = theirs = None
        for block, step in ((own[...], 0), (low[...], 3), (high[...], 1), (far, 2)):
            at = lax.rem(pos[0] + step, NY)
            span = pl.ds(pl.multiple_of(at * units, units), units)
            own_term = times(block, down_own[span, :])
            other_term = times(block, down_other[span, :])
            mine = own_term if mine is None else mine + own_term
            theirs = other_term if theirs is None else theirs + other_term
        store_columns(pos, out, slice(index * rows, (index + 1) * rows), mine, theirs)


def combine_kernel(pos, *refs):
    keep_out, give_out = refs[-2:]
    cols = keep_out.shape[1]
    pairs = len(refs) // 2 - 1
    for out, core in ((give_out, 1 - pos[1]), (keep_out, pos[1])):
        at = pl.ds(pl.multiple_of(core * cols, cols), cols)
        total = None
        for index in range(pairs):
            step = times(refs[2 * index][...], refs[2 * index + 1][:, at])
            total = step if total is None else total + step
        out[...] = total.astype(out.dtype)


def turn(array, step):
    return lax.ppermute(array, "y", [(i, (i + step) % NY) for i in range(NY)])


def ring(block):
    half = block.shape[0] // 2
    low = turn(block, 1)
    high = turn(block, -1)
    return block, low, high, turn(low[:half], 1), turn(high[half:], -1)


def body(tokens, norm_gain, router, routes, w_gate, w_up, w_down):
    count, width = tokens.shape
    quarter = width // NY
    units = 2 * w_gate.shape[1]
    ff = w_down.shape[1]
    cols = w_down.shape[2]
    sds = jax.ShapeDtypeStruct
    pos = jnp.stack([lax.axis_index("y"), lax.axis_index("c")]).astype(jnp.int32)
    turned = routes.T
    sizes = [N_EXP * size for _, size in CHUNKS]

    gain = norm_gain[None, :]
    part, first_rows = pl.pallas_call(
        first_kernel,
        out_shape=(sds((count, quarter), BF16), sds((sizes[0], quarter), BF16)),
        in_specs=[SMEM] + [VMEM] * 3,
        out_specs=(VMEM, VMEM),
        compiler_params=params(16),
        cost_estimate=cost(2 * count * sizes[0] * quarter, count * width * 2),
    )(pos, tokens, gain, turned)
    received = [lax.all_to_all(first_rows, ("x", "z"), 0, 0, tiled=True)]
    later_rows = pl.pallas_call(
        later_kernel,
        out_shape=tuple(sds((size, quarter), BF16) for size in sizes[1:]),
        in_specs=[SMEM] + [VMEM] * 2,
        out_specs=(VMEM,) * (len(CHUNKS) - 1),
        compiler_params=params(16),
        cost_estimate=cost(2 * count * sum(sizes) * quarter, sum(sizes) * quarter * 2),
    )(pos, part, turned)
    arrays = (w_gate, w_up, w_down)
    sent, own = [
        [lax.dynamic_index_in_dim(array, core, 0, keepdims=False) for array in arrays]
        for core in (1 - pos[1], pos[1])
    ]
    *sent, received[0] = lax.optimization_barrier((*sent, received[0]))
    *own, received[0] = lax.optimization_barrier((*own, received[0]))
    others = [lax.ppermute(array, "c", [(0, 1), (1, 0)]) for array in sent]
    for rows in later_rows:
        rows, received[-1] = lax.optimization_barrier((rows, received[-1]))
        received.append(lax.all_to_all(rows, ("x", "z"), 0, 0, tiled=True))
    tokens, router, received[0] = lax.optimization_barrier((tokens, router, received[0]))
    mixes = pl.pallas_call(
        mix_kernel,
        out_shape=tuple(sds((count, size), BF16) for size in sizes),
        in_specs=[SMEM] + [VMEM] * 4,
        out_specs=(VMEM,) * len(CHUNKS),
        compiler_params=params(16),
        cost_estimate=cost(2 * count * width * 64, count * width * 2),
    )(pos, tokens, gain, router, turned)

    returned = []
    done = []
    for index, size in enumerate(sizes):
        mine = received[index]
        if index == 0:
            inputs = ring(mine)
        else:
            if index == 2:
                mine, *_ = lax.optimization_barrier((mine, *done))
            blocks = lax.all_gather(mine, "y", axis=0)
            if index == 1:
                blocks, returned[0] = lax.optimization_barrier((blocks, returned[0]))
                done.append(blocks)
            inputs = (blocks,)
        pieces = []
        for half in range(size // PIECE):
            hidden = pl.pallas_call(
                functools.partial(hidden_kernel, half) if index else hidden_ring_kernel,
                out_shape=sds((PIECE, units), BF16),
                in_specs=[SMEM] + [VMEM] * (4 + len(inputs)),
                out_specs=VMEM,
                compiler_params=params(24),
                cost_estimate=cost(
                    4 * PIECE * width * units, 4 * units * width + 2 * PIECE * width
                ),
            )(pos, *inputs, own[0], others[0], own[1], others[1])
            if index == 0:
                received[1], hidden = lax.optimization_barrier((received[1], hidden))
            if size > PIECE:
                pieces.extend(ring(hidden))
            else:
                pieces.append(lax.all_gather(hidden, "y", axis=0))
        result = pl.pallas_call(
            down_ring_kernel if size > PIECE else down_kernel,
            out_shape=sds((size, NC * cols), BF16),
            in_specs=[SMEM] + [VMEM] * (2 + len(pieces)),
            out_specs=VMEM,
            compiler_params=params(24),
            cost_estimate=cost(
                2 * size * ff * NC * cols, 2 * ff * NC * cols + 2 * size * NC * cols
            ),
        )(pos, own[2], others[2], *pieces)
        if index == 0:
            result, received[-1] = lax.optimization_barrier((result, received[-1]))
            done.append(result)
        returned.append(lax.all_to_all(result, ("x", "z"), 0, 0, tiled=True))

    total = None
    last = len(CHUNKS) - 1
    for group in (range(last), range(last, last + 1)):
        keep, give = pl.pallas_call(
            combine_kernel,
            out_shape=(sds((count, cols), F32), sds((count, cols), BF16)),
            in_specs=[SMEM] + [VMEM] * (2 * len(group)),
            out_specs=(VMEM, VMEM),
            compiler_params=params(16),
            cost_estimate=cost(4 * count * cols * 512, 1 << 20),
        )(pos, *[item for i in group for item in (mixes[i], returned[i])])
        give = lax.ppermute(give, "c", [(0, 1), (1, 0)])
        share = keep + give.astype(F32)
        total = share if total is None else total + share
    return total.astype(BF16)


def solution(mesh):
    grid = Mesh(mesh.devices.reshape(NY, NC, NX, NZ), ("y", "c", "x", "z"))
    enc, exp = ("y", "c"), ("x", "z")
    return jax.shard_map(
        body,
        mesh=grid,
        in_specs=(
            P(exp, None),
            P(),
            P(),
            P(exp, None),
            P(exp, enc, None),
            P(exp, enc, None),
            P(exp, None, enc),
        ),
        out_specs=P(exp, enc),
        check_vma=False,
    )
```

```python
import functools

import jax
import jax.numpy as jnp
from jax import lax
from jax.experimental import pallas as pl
from jax.experimental.pallas import tpu as pltpu
from jax.sharding import Mesh, PartitionSpec as P

EPS = 1e-06
F32 = jnp.float32
BF16 = jnp.bfloat16
NY, NC, NX, NZ = 4, 2, 4, 8
N_EXP = NX * NZ
CHUNKS = ((0, 16), (16, 16))

VMEM = pl.BlockSpec(memory_space=pltpu.VMEM)
SMEM = pl.BlockSpec(memory_space=pltpu.SMEM)


def by_rows(left, right):
    return lax.dot_general(
        left, right, (((1,), (1,)), ((), ())), preferred_element_type=F32
    )


def times(left, right):
    return jnp.dot(left, right, preferred_element_type=F32)


def params(mib):
    return pltpu.CompilerParams(vmem_limit_bytes=mib << 20)


def cost(flops, moved):
    return pl.CostEstimate(flops=flops, bytes_accessed=moved, transcendentals=0)


def places(names, core):
    tokens = names.shape[1]
    expert = core.astype(F32) + 2.0 * lax.broadcasted_iota(
        jnp.int32, (N_EXP, tokens), 0
    ).astype(F32)
    hits = [names[k : k + 1, :] == expert for k in range(8)]
    named = hits[0]
    for hit in hits[1:]:
        named = named | hit
    row = lax.broadcasted_iota(jnp.int32, (tokens, tokens), 0)
    col = lax.broadcasted_iota(jnp.int32, (tokens, tokens), 1)
    earlier = jnp.where(row < col, 1.0, 0.0).astype(BF16)
    before = times(jnp.where(named, 1.0, 0.0).astype(BF16), earlier)
    return hits, jnp.where(named, before, -1.0)


def spread(place, values, first, size):
    tokens = place.shape[1]
    slot = lax.broadcasted_iota(jnp.int32, (size, tokens), 0) + first
    slot = slot.astype(F32)
    return jnp.concatenate(
        [
            jnp.where(place[d : d + 1, :] == slot, values[d : d + 1, :], 0.0)
            for d in range(N_EXP)
        ],
        axis=0,
    )


def pick(names, part, chunk, core):
    _, place = places(names, core)
    picks = spread(place, jnp.ones_like(place), *chunk).astype(BF16)
    return times(picks, part).astype(BF16)


def first_kernel(pos, tokens, gain, routes, part_out, rows_out):
    values = tokens[...].astype(F32)
    count, width = values.shape
    squares = jnp.sum(values * values, axis=1, keepdims=True)
    inverse = lax.rsqrt(squares / width + EPS)
    quarter = width // NY
    cols = pl.ds(pl.multiple_of(pos[0] * quarter, quarter), quarter)
    mine = (tokens[:, cols].astype(F32) * gain[:, cols].astype(F32)).astype(BF16)
    part = (mine.astype(F32) * inverse).astype(BF16)
    part_out[...] = part
    rows_out[...] = pick(routes[...].astype(F32), part, CHUNKS[0], pos[1])


def later_kernel(pos, part, routes, *rows_out):
    for chunk, out in zip(CHUNKS[1:], rows_out):
        out[...] = pick(routes[...].astype(F32), part[...], chunk, pos[1])


def mix_kernel(pos, tokens, gain, router, routes, *mix_out):
    values = tokens[...].astype(F32)
    count, width = values.shape
    scaled = (values * gain[...].astype(F32)).astype(BF16)
    squares = jnp.sum(values * values, axis=1, keepdims=True)
    inverse = lax.rsqrt(squares / width + EPS)
    turned = jnp.transpose(jnp.broadcast_to(inverse, (count, 128)))
    logits = by_rows(router[...], scaled) * turned[0:1, :]
    expert = lax.broadcasted_iota(jnp.int32, logits.shape, 0).astype(F32)
    names = routes[...].astype(F32)
    chosen = [
        jnp.sum(jnp.where(names[k : k + 1, :] == expert, logits, 0.0), axis=0, keepdims=True)
        for k in range(8)
    ]
    raised = jnp.exp(jnp.concatenate(chosen, axis=0))
    weights = raised / jnp.sum(raised, axis=0, keepdims=True)
    hits, place = places(names, pos[1])
    dense = jnp.zeros_like(place)
    for k in range(8):
        dense = dense + jnp.where(hits[k], weights[k : k + 1, :], 0.0)
    for (first, size), out in zip(CHUNKS, mix_out):
        out[...] = jnp.transpose(spread(place, dense, first, size)).astype(BF16)


def activate(pos, sums):
    units = sums.shape[0] // 4
    gate_own, up_own, gate_other, up_other = [
        sums[index * units : (index + 1) * units] for index in range(4)
    ]
    own = gate_own / (1.0 + jnp.exp(-gate_own)) * up_own
    other = gate_other / (1.0 + jnp.exp(-gate_other)) * up_other
    low = jnp.where(pos[1] == 0, own, other)
    high = jnp.where(pos[1] == 0, other, own)
    return jnp.transpose(jnp.concatenate([low, high], axis=0)).astype(BF16)


def hidden_kernel(pos, blocks, gate_own, gate_other, up_own, up_other, out):
    quarter = blocks.shape[2]
    total = None
    for y in range(NY):
        cols = slice(y * quarter, (y + 1) * quarter)
        weights = jnp.concatenate(
            [weight[:, cols] for weight in (gate_own, up_own, gate_other, up_other)], axis=0
        )
        term = by_rows(weights, blocks[y])
        total = term if y == 0 else total + term
    out[...] = activate(pos, total)


def hidden_ring_kernel(
    pos, own, low, high, far_top, far_bottom, gate_own, gate_other, up_own, up_other, out
):
    quarter = own.shape[1]
    far = jnp.concatenate([far_top[...], far_bottom[...]], axis=0)
    total = None
    for block, step in ((own[...], 0), (low[...], 3), (high[...], 1), (far, 2)):
        at = lax.rem(pos[0] + step, NY)
        cols = pl.ds(pl.multiple_of(at * quarter, quarter), quarter)
        weights = jnp.concatenate(
            [weight[:, cols] for weight in (gate_own, up_own, gate_other, up_other)], axis=0
        )
        term = by_rows(weights, block)
        total = term if total is None else total + term
    out[...] = activate(pos, total)


def down_kernel(pos, down_own, down_other, own, low, high, far_top, far_bottom, out):
    units = own.shape[1]
    cols = down_own.shape[1]
    far = jnp.concatenate([far_top[...], far_bottom[...]], axis=0)
    mine = theirs = None
    for block, step in ((own[...], 0), (low[...], 3), (high[...], 1), (far, 2)):
        at = lax.rem(pos[0] + step, NY)
        span = pl.ds(pl.multiple_of(at * units, units), units)
        own_term = times(block, down_own[span, :])
        other_term = times(block, down_other[span, :])
        mine = own_term if mine is None else mine + own_term
        theirs = other_term if theirs is None else theirs + other_term
    for core, total in ((pos[1], mine), (1 - pos[1], theirs)):
        out[:, pl.ds(pl.multiple_of(core * cols, cols), cols)] = total.astype(BF16)


def combine_kernel(pos, *refs):
    keep_out, give_out = refs[-2:]
    cols = keep_out.shape[1]
    pairs = len(refs) // 2 - 1
    for out, core in ((give_out, 1 - pos[1]), (keep_out, pos[1])):
        at = pl.ds(pl.multiple_of(core * cols, cols), cols)
        total = None
        for index in range(pairs):
            step = times(refs[2 * index][...], refs[2 * index + 1][:, at])
            total = step if total is None else total + step
        out[...] = total.astype(out.dtype)


def turn(array, step):
    return lax.ppermute(array, "y", [(i, (i + step) % NY) for i in range(NY)])


def ring_start(block):
    return turn(block, 1), turn(block, -1)


def ring_end(block, low, high):
    half = block.shape[0] // 2
    return block, low, high, turn(low[:half], 1), turn(high[half:], -1)


def ring(block):
    return ring_end(block, *ring_start(block))


def body(tokens, norm_gain, router, routes, w_gate, w_up, w_down):
    count, width = tokens.shape
    quarter = width // NY
    units = 2 * w_gate.shape[1]
    ff = w_down.shape[1]
    cols = w_down.shape[2]
    sds = jax.ShapeDtypeStruct
    pos = jnp.stack([lax.axis_index("y"), lax.axis_index("c")]).astype(jnp.int32)
    turned = routes.T
    sizes = [N_EXP * size for _, size in CHUNKS]

    gain = norm_gain[None, :]
    part, first_rows = pl.pallas_call(
        first_kernel,
        out_shape=(sds((count, quarter), BF16), sds((sizes[0], quarter), BF16)),
        in_specs=[SMEM] + [VMEM] * 3,
        out_specs=(VMEM, VMEM),
        compiler_params=params(16),
        cost_estimate=cost(2 * count * sizes[0] * quarter, count * width * 2),
    )(pos, tokens, gain, turned)
    received = [lax.all_to_all(first_rows, ("x", "z"), 0, 0, tiled=True)]
    later_rows = pl.pallas_call(
        later_kernel,
        out_shape=tuple(sds((size, quarter), BF16) for size in sizes[1:]),
        in_specs=[SMEM] + [VMEM] * 2,
        out_specs=(VMEM,) * (len(CHUNKS) - 1),
        compiler_params=params(16),
        cost_estimate=cost(2 * count * sum(sizes) * quarter, sum(sizes) * quarter * 2),
    )(pos, part, turned)
    arrays = (w_gate, w_up, w_down)
    sent, own = [
        [lax.dynamic_index_in_dim(array, core, 0, keepdims=False) for array in arrays]
        for core in (1 - pos[1], pos[1])
    ]
    *sent, received[0] = lax.optimization_barrier((*sent, received[0]))
    *own, received[0] = lax.optimization_barrier((*own, received[0]))
    others = [lax.ppermute(array, "c", [(0, 1), (1, 0)]) for array in sent]
    for rows in later_rows:
        rows, received[-1] = lax.optimization_barrier((rows, received[-1]))
        received.append(lax.all_to_all(rows, ("x", "z"), 0, 0, tiled=True))
    tokens, router, received[0] = lax.optimization_barrier((tokens, router, received[0]))
    mixes = pl.pallas_call(
        mix_kernel,
        out_shape=tuple(sds((count, size), BF16) for size in sizes),
        in_specs=[SMEM] + [VMEM] * 4,
        out_specs=(VMEM,) * len(CHUNKS),
        compiler_params=params(16),
        cost_estimate=cost(2 * count * width * 64, count * width * 2),
    )(pos, tokens, gain, router, turned)

    returned = []
    low, high = ring_start(received[1])
    gathered = lax.all_gather(received[0], "y", axis=0)
    gathered, low, high = lax.optimization_barrier((gathered, low, high))
    later = ring_end(received[1], low, high)
    for index, size in enumerate(sizes):
        inputs = later if index else (gathered,)
        if index:
            *inputs, first_hidden = lax.optimization_barrier((*inputs, first_hidden))
        hidden = pl.pallas_call(
            hidden_ring_kernel if index else hidden_kernel,
            out_shape=sds((size, units), BF16),
            in_specs=[SMEM] + [VMEM] * (4 + len(inputs)),
            out_specs=VMEM,
            compiler_params=params(16),
            cost_estimate=cost(4 * size * width * units, 4 * units * width + 2 * size * width),
        )(pos, *inputs, own[0], others[0], own[1], others[1])
        first_hidden = hidden
        pieces = ring(hidden)
        if index == 0:
            mixed = lax.optimization_barrier((*pieces, *later))
            pieces, later = mixed[:5], mixed[5:]
        else:
            *pieces, first_result = lax.optimization_barrier((*pieces, first_result))
        result = pl.pallas_call(
            down_kernel,
            out_shape=sds((size, NC * cols), BF16),
            in_specs=[SMEM] + [VMEM] * 7,
            out_specs=VMEM,
            compiler_params=params(16),
            cost_estimate=cost(
                2 * size * ff * NC * cols, 2 * ff * NC * cols + 2 * size * NC * cols
            ),
        )(pos, own[2], others[2], *pieces)
        first_result = result
        returned.append(lax.all_to_all(result, ("x", "z"), 0, 0, tiled=True))

    total = None
    last = len(CHUNKS) - 1
    for group in (range(last), range(last, last + 1)):
        keep, give = pl.pallas_call(
            combine_kernel,
            out_shape=(sds((count, cols), F32), sds((count, cols), BF16)),
            in_specs=[SMEM] + [VMEM] * (2 * len(group)),
            out_specs=(VMEM, VMEM),
            compiler_params=params(16),
            cost_estimate=cost(4 * count * cols * 512, 1 << 20),
        )(pos, *[item for i in group for item in (mixes[i], returned[i])])
        give = lax.ppermute(give, "c", [(0, 1), (1, 0)])
        share = keep + give.astype(F32)
        total = share if total is None else total + share
    return total.astype(BF16)


def solution(mesh):
    grid = Mesh(mesh.devices.reshape(NY, NC, NX, NZ), ("y", "c", "x", "z"))
    enc, exp = ("y", "c"), ("x", "z")
    return jax.shard_map(
        body,
        mesh=grid,
        in_specs=(
            P(exp, None),
            P(),
            P(),
            P(exp, None),
            P(exp, enc, None),
            P(exp, enc, None),
            P(exp, None, enc),
        ),
        out_specs=P(exp, enc),
        check_vma=False,
    )
```

```python
import functools

import jax
import jax.numpy as jnp
from jax import lax
from jax.experimental import pallas as pl
from jax.experimental.pallas import tpu as pltpu
from jax.sharding import Mesh, PartitionSpec as P

EPS = 1e-06
F32 = jnp.float32
BF16 = jnp.bfloat16
NY, NC, NX, NZ = 4, 2, 4, 8
N_EXP = NX * NZ
CHUNKS = ((0, 8), (8, 16), (24, 8))
PIECE = 256

VMEM = pl.BlockSpec(memory_space=pltpu.VMEM)
SMEM = pl.BlockSpec(memory_space=pltpu.SMEM)


def by_rows(left, right):
    return lax.dot_general(
        left, right, (((1,), (1,)), ((), ())), preferred_element_type=F32
    )


def times(left, right):
    return jnp.dot(left, right, preferred_element_type=F32)


def params(mib):
    return pltpu.CompilerParams(vmem_limit_bytes=mib << 20)


def cost(flops, moved):
    return pl.CostEstimate(flops=flops, bytes_accessed=moved, transcendentals=0)


def places(names, core):
    tokens = names.shape[1]
    expert = core.astype(F32) + 2.0 * lax.broadcasted_iota(
        jnp.int32, (N_EXP, tokens), 0
    ).astype(F32)
    hits = [names[k : k + 1, :] == expert for k in range(8)]
    named = hits[0]
    for hit in hits[1:]:
        named = named | hit
    row = lax.broadcasted_iota(jnp.int32, (tokens, tokens), 0)
    col = lax.broadcasted_iota(jnp.int32, (tokens, tokens), 1)
    earlier = jnp.where(row < col, 1.0, 0.0).astype(BF16)
    before = times(jnp.where(named, 1.0, 0.0).astype(BF16), earlier)
    return hits, jnp.where(named, before, -1.0)


def spread(place, values, first, size):
    tokens = place.shape[1]
    slot = lax.broadcasted_iota(jnp.int32, (size, tokens), 0) + first
    slot = slot.astype(F32)
    return jnp.concatenate(
        [
            jnp.where(place[d : d + 1, :] == slot, values[d : d + 1, :], 0.0)
            for d in range(N_EXP)
        ],
        axis=0,
    )


def pick(names, part, chunk, core):
    _, place = places(names, core)
    picks = spread(place, jnp.ones_like(place), *chunk).astype(BF16)
    return times(picks, part).astype(BF16)


def first_kernel(pos, tokens, gain, routes, part_out, rows_out):
    values = tokens[...].astype(F32)
    count, width = values.shape
    squares = jnp.sum(values * values, axis=1, keepdims=True)
    inverse = lax.rsqrt(squares / width + EPS)
    quarter = width // NY
    cols = pl.ds(pl.multiple_of(pos[0] * quarter, quarter), quarter)
    mine = (tokens[:, cols].astype(F32) * gain[:, cols].astype(F32)).astype(BF16)
    part = (mine.astype(F32) * inverse).astype(BF16)
    part_out[...] = part
    rows_out[...] = pick(routes[...].astype(F32), part, CHUNKS[0], pos[1])


def later_kernel(pos, part, routes, *rows_out):
    for chunk, out in zip(CHUNKS[1:], rows_out):
        out[...] = pick(routes[...].astype(F32), part[...], chunk, pos[1])


def mix_kernel(pos, tokens, gain, router, routes, *mix_out):
    values = tokens[...].astype(F32)
    count, width = values.shape
    scaled = (values * gain[...].astype(F32)).astype(BF16)
    squares = jnp.sum(values * values, axis=1, keepdims=True)
    inverse = lax.rsqrt(squares / width + EPS)
    turned = jnp.transpose(jnp.broadcast_to(inverse, (count, 128)))
    logits = by_rows(router[...], scaled) * turned[0:1, :]
    expert = lax.broadcasted_iota(jnp.int32, logits.shape, 0).astype(F32)
    names = routes[...].astype(F32)
    chosen = [
        jnp.sum(jnp.where(names[k : k + 1, :] == expert, logits, 0.0), axis=0, keepdims=True)
        for k in range(8)
    ]
    raised = jnp.exp(jnp.concatenate(chosen, axis=0))
    weights = raised / jnp.sum(raised, axis=0, keepdims=True)
    hits, place = places(names, pos[1])
    dense = jnp.zeros_like(place)
    for k in range(8):
        dense = dense + jnp.where(hits[k], weights[k : k + 1, :], 0.0)
    for (first, size), out in zip(CHUNKS, mix_out):
        out[...] = jnp.transpose(spread(place, dense, first, size)).astype(BF16)


def activate(pos, sums):
    units = sums.shape[0] // 4
    gate_own, up_own, gate_other, up_other = [
        sums[index * units : (index + 1) * units] for index in range(4)
    ]
    own = gate_own / (1.0 + jnp.exp(-gate_own)) * up_own
    other = gate_other / (1.0 + jnp.exp(-gate_other)) * up_other
    low = jnp.where(pos[1] == 0, own, other)
    high = jnp.where(pos[1] == 0, other, own)
    return jnp.transpose(jnp.concatenate([low, high], axis=0)).astype(BF16)


def hidden_kernel(half, pos, blocks, gate_own, gate_other, up_own, up_other, out):
    quarter = blocks.shape[2]
    rows = slice(half * PIECE, (half + 1) * PIECE)
    total = None
    for y in range(NY):
        cols = slice(y * quarter, (y + 1) * quarter)
        weights = jnp.concatenate(
            [weight[:, cols] for weight in (gate_own, up_own, gate_other, up_other)], axis=0
        )
        term = by_rows(weights, blocks[y, rows, :])
        total = term if y == 0 else total + term
    out[...] = activate(pos, total)


def store_columns(pos, out, at, own, other):
    cols = own.shape[1]
    for core, total in ((pos[1], own), (1 - pos[1], other)):
        out[at, pl.ds(pl.multiple_of(core * cols, cols), cols)] = total.astype(BF16)


def down_kernel(pos, down_own, down_other, blocks, out):
    rows, units = blocks.shape[1:]
    own = other = None
    for y in range(NY):
        span = slice(y * units, (y + 1) * units)
        own_term = times(blocks[y], down_own[span, :])
        other_term = times(blocks[y], down_other[span, :])
        own = own_term if y == 0 else own + own_term
        other = other_term if y == 0 else other + other_term
    store_columns(pos, out, slice(0, rows), own, other)


def down_ring_kernel(pos, down_own, down_other, *refs):
    out = refs[-1]
    for index in range(len(refs) // 5):
        own, low, high, far_top, far_bottom = refs[5 * index : 5 * index + 5]
        rows, units = own.shape
        far = jnp.concatenate([far_top[...], far_bottom[...]], axis=0)
        mine = theirs = None
        for block, step in ((own[...], 0), (low[...], 3), (high[...], 1), (far, 2)):
            at = lax.rem(pos[0] + step, NY)
            span = pl.ds(pl.multiple_of(at * units, units), units)
            own_term = times(block, down_own[span, :])
            other_term = times(block, down_other[span, :])
            mine = own_term if mine is None else mine + own_term
            theirs = other_term if theirs is None else theirs + other_term
        store_columns(pos, out, slice(index * rows, (index + 1) * rows), mine, theirs)


def combine_kernel(pos, *refs):
    keep_out, give_out = refs[-2:]
    cols = keep_out.shape[1]
    pairs = len(refs) // 2 - 1
    for out, core in ((give_out, 1 - pos[1]), (keep_out, pos[1])):
        at = pl.ds(pl.multiple_of(core * cols, cols), cols)
        total = None
        for index in range(pairs):
            step = times(refs[2 * index][...], refs[2 * index + 1][:, at])
            total = step if total is None else total + step
        out[...] = total.astype(out.dtype)


def turn(array, step):
    return lax.ppermute(array, "y", [(i, (i + step) % NY) for i in range(NY)])


def ring(block):
    half = block.shape[0] // 2
    low = turn(block, 1)
    high = turn(block, -1)
    return block, low, high, turn(low[:half], 1), turn(high[half:], -1)


def body(tokens, norm_gain, router, routes, w_gate, w_up, w_down):
    count, width = tokens.shape
    quarter = width // NY
    units = 2 * w_gate.shape[1]
    ff = w_down.shape[1]
    cols = w_down.shape[2]
    sds = jax.ShapeDtypeStruct
    pos = jnp.stack([lax.axis_index("y"), lax.axis_index("c")]).astype(jnp.int32)
    turned = routes.T
    sizes = [N_EXP * size for _, size in CHUNKS]

    gain = norm_gain[None, :]
    part, first_rows = pl.pallas_call(
        first_kernel,
        out_shape=(sds((count, quarter), BF16), sds((sizes[0], quarter), BF16)),
        in_specs=[SMEM] + [VMEM] * 3,
        out_specs=(VMEM, VMEM),
        compiler_params=params(16),
        cost_estimate=cost(2 * count * sizes[0] * quarter, count * width * 2),
    )(pos, tokens, gain, turned)
    received = [lax.all_to_all(first_rows, ("x", "z"), 0, 0, tiled=True)]
    later_rows = pl.pallas_call(
        later_kernel,
        out_shape=tuple(sds((size, quarter), BF16) for size in sizes[1:]),
        in_specs=[SMEM] + [VMEM] * 2,
        out_specs=(VMEM,) * (len(CHUNKS) - 1),
        compiler_params=params(16),
        cost_estimate=cost(2 * count * sum(sizes) * quarter, sum(sizes) * quarter * 2),
    )(pos, part, turned)
    arrays = (w_gate, w_up, w_down)
    sent, own = [
        [lax.dynamic_index_in_dim(array, core, 0, keepdims=False) for array in arrays]
        for core in (1 - pos[1], pos[1])
    ]
    *sent, received[0] = lax.optimization_barrier((*sent, received[0]))
    *own, received[0] = lax.optimization_barrier((*own, received[0]))
    others = [lax.ppermute(array, "c", [(0, 1), (1, 0)]) for array in sent]
    for rows in later_rows:
        rows, received[-1] = lax.optimization_barrier((rows, received[-1]))
        received.append(lax.all_to_all(rows, ("x", "z"), 0, 0, tiled=True))
    tokens, router, received[0] = lax.optimization_barrier((tokens, router, received[0]))
    mixes = pl.pallas_call(
        mix_kernel,
        out_shape=tuple(sds((count, size), BF16) for size in sizes),
        in_specs=[SMEM] + [VMEM] * 4,
        out_specs=(VMEM,) * len(CHUNKS),
        compiler_params=params(16),
        cost_estimate=cost(2 * count * width * 64, count * width * 2),
    )(pos, tokens, gain, router, turned)

    returned = []
    done = []
    for index, size in enumerate(sizes):
        mine = received[index]
        if index:
            before = [done[i][j] for i, j in ((index - 1, 0), (index - 2, 1)) if i >= 0]
            mine, *before = lax.optimization_barrier((mine, *before))
        blocks = lax.all_gather(mine, "y", axis=0)
        if index == 1:
            blocks, returned[0] = lax.optimization_barrier((blocks, returned[0]))
        pieces = []
        for half in range(size // PIECE):
            hidden = pl.pallas_call(
                functools.partial(hidden_kernel, half),
                out_shape=sds((PIECE, units), BF16),
                in_specs=[SMEM] + [VMEM] * 5,
                out_specs=VMEM,
                compiler_params=params(16),
                cost_estimate=cost(
                    4 * PIECE * width * units, 4 * units * width + 2 * PIECE * width
                ),
            )(pos, blocks, own[0], others[0], own[1], others[1])
            if size > PIECE:
                pieces.extend(ring(hidden))
            else:
                pieces.append(lax.all_gather(hidden, "y", axis=0))
        result = pl.pallas_call(
            down_ring_kernel if size > PIECE else down_kernel,
            out_shape=sds((size, NC * cols), BF16),
            in_specs=[SMEM] + [VMEM] * (2 + len(pieces)),
            out_specs=VMEM,
            compiler_params=params(16),
            cost_estimate=cost(
                2 * size * ff * NC * cols, 2 * ff * NC * cols + 2 * size * NC * cols
            ),
        )(pos, own[2], others[2], *pieces)
        if index == 0:
            result, received[-1] = lax.optimization_barrier((result, received[-1]))
        done.append((blocks, result))
        returned.append(lax.all_to_all(result, ("x", "z"), 0, 0, tiled=True))

    total = None
    last = len(CHUNKS) - 1
    for group in (range(last), range(last, last + 1)):
        keep, give = pl.pallas_call(
            combine_kernel,
            out_shape=(sds((count, cols), F32), sds((count, cols), BF16)),
            in_specs=[SMEM] + [VMEM] * (2 * len(group)),
            out_specs=(VMEM, VMEM),
            compiler_params=params(16),
            cost_estimate=cost(4 * count * cols * 512, 1 << 20),
        )(pos, *[item for i in group for item in (mixes[i], returned[i])])
        give = lax.ppermute(give, "c", [(0, 1), (1, 0)])
        share = keep + give.astype(F32)
        total = share if total is None else total + share
    return total.astype(BF16)


def solution(mesh):
    grid = Mesh(mesh.devices.reshape(NY, NC, NX, NZ), ("y", "c", "x", "z"))
    enc, exp = ("y", "c"), ("x", "z")
    return jax.shard_map(
        body,
        mesh=grid,
        in_specs=(
            P(exp, None),
            P(),
            P(),
            P(exp, None),
            P(exp, enc, None),
            P(exp, enc, None),
            P(exp, None, enc),
        ),
        out_specs=P(exp, enc),
        check_vma=False,
    )
```

```python
import functools

import jax
import jax.numpy as jnp
from jax import lax
from jax.experimental import pallas as pl
from jax.experimental.pallas import tpu as pltpu
from jax.sharding import Mesh, PartitionSpec as P

EPS = 1e-06
F32 = jnp.float32
BF16 = jnp.bfloat16
NY, NC, NX, NZ = 4, 2, 4, 8
N_EXP = NX * NZ
CHUNKS = ((0, 8), (8, 16), (24, 8))
PIECE = 256

VMEM = pl.BlockSpec(memory_space=pltpu.VMEM)
SMEM = pl.BlockSpec(memory_space=pltpu.SMEM)


def by_rows(left, right):
    return lax.dot_general(
        left, right, (((1,), (1,)), ((), ())), preferred_element_type=F32
    )


def times(left, right):
    return jnp.dot(left, right, preferred_element_type=F32)


def params(mib):
    return pltpu.CompilerParams(vmem_limit_bytes=mib << 20)


def cost(flops, moved):
    return pl.CostEstimate(flops=flops, bytes_accessed=moved, transcendentals=0)


def places(names, core):
    tokens = names.shape[1]
    expert = core.astype(F32) + 2.0 * lax.broadcasted_iota(
        jnp.int32, (N_EXP, tokens), 0
    ).astype(F32)
    hits = [names[k : k + 1, :] == expert for k in range(8)]
    named = hits[0]
    for hit in hits[1:]:
        named = named | hit
    row = lax.broadcasted_iota(jnp.int32, (tokens, tokens), 0)
    col = lax.broadcasted_iota(jnp.int32, (tokens, tokens), 1)
    earlier = jnp.where(row < col, 1.0, 0.0).astype(BF16)
    before = times(jnp.where(named, 1.0, 0.0).astype(BF16), earlier)
    return hits, jnp.where(named, before, -1.0)


def spread(place, values, first, size):
    tokens = place.shape[1]
    slot = lax.broadcasted_iota(jnp.int32, (size, tokens), 0) + first
    slot = slot.astype(F32)
    return jnp.concatenate(
        [
            jnp.where(place[d : d + 1, :] == slot, values[d : d + 1, :], 0.0)
            for d in range(N_EXP)
        ],
        axis=0,
    )


def pick(names, part, chunk, core):
    _, place = places(names, core)
    picks = spread(place, jnp.ones_like(place), *chunk).astype(BF16)
    return times(picks, part).astype(BF16)


def first_kernel(pos, tokens, gain, routes, part_out, rows_out):
    values = tokens[...].astype(F32)
    count, width = values.shape
    squares = jnp.sum(values * values, axis=1, keepdims=True)
    inverse = lax.rsqrt(squares / width + EPS)
    quarter = width // NY
    cols = pl.ds(pl.multiple_of(pos[0] * quarter, quarter), quarter)
    mine = (tokens[:, cols].astype(F32) * gain[:, cols].astype(F32)).astype(BF16)
    part = (mine.astype(F32) * inverse).astype(BF16)
    part_out[...] = part
    rows_out[...] = pick(routes[...].astype(F32), part, CHUNKS[0], pos[1])


def later_kernel(pos, part, routes, *rows_out):
    for chunk, out in zip(CHUNKS[1:], rows_out):
        out[...] = pick(routes[...].astype(F32), part[...], chunk, pos[1])


def mix_kernel(pos, tokens, gain, router, routes, *mix_out):
    values = tokens[...].astype(F32)
    count, width = values.shape
    scaled = (values * gain[...].astype(F32)).astype(BF16)
    squares = jnp.sum(values * values, axis=1, keepdims=True)
    inverse = lax.rsqrt(squares / width + EPS)
    turned = jnp.transpose(jnp.broadcast_to(inverse, (count, 128)))
    logits = by_rows(router[...], scaled) * turned[0:1, :]
    expert = lax.broadcasted_iota(jnp.int32, logits.shape, 0).astype(F32)
    names = routes[...].astype(F32)
    chosen = [
        jnp.sum(jnp.where(names[k : k + 1, :] == expert, logits, 0.0), axis=0, keepdims=True)
        for k in range(8)
    ]
    raised = jnp.exp(jnp.concatenate(chosen, axis=0))
    weights = raised / jnp.sum(raised, axis=0, keepdims=True)
    hits, place = places(names, pos[1])
    dense = jnp.zeros_like(place)
    for k in range(8):
        dense = dense + jnp.where(hits[k], weights[k : k + 1, :], 0.0)
    for (first, size), out in zip(CHUNKS, mix_out):
        out[...] = jnp.transpose(spread(place, dense, first, size)).astype(BF16)


def activate(pos, sums):
    units = sums.shape[0] // 4
    gate_own, up_own, gate_other, up_other = [
        sums[index * units : (index + 1) * units] for index in range(4)
    ]
    own = gate_own / (1.0 + jnp.exp(-gate_own)) * up_own
    other = gate_other / (1.0 + jnp.exp(-gate_other)) * up_other
    low = jnp.where(pos[1] == 0, own, other)
    high = jnp.where(pos[1] == 0, other, own)
    return jnp.transpose(jnp.concatenate([low, high], axis=0)).astype(BF16)


def hidden_kernel(
    half, pos, blocks, gate_own, up_own, gate_other, up_other, out, gate_held, up_held, sems
):
    fetches = [
        pltpu.make_async_copy(gate_other, gate_held, sems.at[0]),
        pltpu.make_async_copy(up_other, up_held, sems.at[1]),
    ]
    for fetch in fetches:
        fetch.start()
    quarter = blocks.shape[2]
    rows = slice(half * PIECE, (half + 1) * PIECE)
    totals = []
    for pair in ((gate_own, up_own), (gate_held, up_held)):
        if totals:
            for fetch in fetches:
                fetch.wait()
        total = None
        for y in range(NY):
            cols = slice(y * quarter, (y + 1) * quarter)
            weights = jnp.concatenate([weight[:, cols] for weight in pair], axis=0)
            term = by_rows(weights, blocks[y, rows, :])
            total = term if y == 0 else total + term
        totals.append(total)
    out[...] = activate(pos, jnp.concatenate(totals, axis=0))


def store_columns(pos, out, at, own, other):
    cols = own.shape[1]
    for core, total in ((pos[1], own), (1 - pos[1], other)):
        out[at, pl.ds(pl.multiple_of(core * cols, cols), cols)] = total.astype(BF16)


def down_kernel(pos, down_own, down_other, blocks, out):
    rows, units = blocks.shape[1:]
    own = other = None
    for y in range(NY):
        span = slice(y * units, (y + 1) * units)
        own_term = times(blocks[y], down_own[span, :])
        other_term = times(blocks[y], down_other[span, :])
        own = own_term if y == 0 else own + own_term
        other = other_term if y == 0 else other + other_term
    store_columns(pos, out, slice(0, rows), own, other)


def down_ring_kernel(pos, down_own, down_other, *refs):
    out = refs[-1]
    for index in range(len(refs) // 5):
        own, low, high, far_top, far_bottom = refs[5 * index : 5 * index + 5]
        rows, units = own.shape
        far = jnp.concatenate([far_top[...], far_bottom[...]], axis=0)
        mine = theirs = None
        for block, step in ((own[...], 0), (low[...], 3), (high[...], 1), (far, 2)):
            at = lax.rem(pos[0] + step, NY)
            span = pl.ds(pl.multiple_of(at * units, units), units)
            own_term = times(block, down_own[span, :])
            other_term = times(block, down_other[span, :])
            mine = own_term if mine is None else mine + own_term
            theirs = other_term if theirs is None else theirs + other_term
        store_columns(pos, out, slice(index * rows, (index + 1) * rows), mine, theirs)


def combine_kernel(pos, *refs):
    keep_out, give_out = refs[-2:]
    cols = keep_out.shape[1]
    pairs = len(refs) // 2 - 1
    for out, core in ((give_out, 1 - pos[1]), (keep_out, pos[1])):
        at = pl.ds(pl.multiple_of(core * cols, cols), cols)
        total = None
        for index in range(pairs):
            step = times(refs[2 * index][...], refs[2 * index + 1][:, at])
            total = step if total is None else total + step
        out[...] = total.astype(out.dtype)


def turn(array, step):
    return lax.ppermute(array, "y", [(i, (i + step) % NY) for i in range(NY)])


def ring(block):
    half = block.shape[0] // 2
    low = turn(block, 1)
    high = turn(block, -1)
    return block, low, high, turn(low[:half], 1), turn(high[half:], -1)


def body(tokens, norm_gain, router, routes, w_gate, w_up, w_down):
    count, width = tokens.shape
    quarter = width // NY
    units = 2 * w_gate.shape[1]
    ff = w_down.shape[1]
    cols = w_down.shape[2]
    sds = jax.ShapeDtypeStruct
    pos = jnp.stack([lax.axis_index("y"), lax.axis_index("c")]).astype(jnp.int32)
    turned = routes.T
    sizes = [N_EXP * size for _, size in CHUNKS]

    gain = norm_gain[None, :]
    part, first_rows = pl.pallas_call(
        first_kernel,
        out_shape=(sds((count, quarter), BF16), sds((sizes[0], quarter), BF16)),
        in_specs=[SMEM] + [VMEM] * 3,
        out_specs=(VMEM, VMEM),
        compiler_params=params(16),
        cost_estimate=cost(2 * count * sizes[0] * quarter, count * width * 2),
    )(pos, tokens, gain, turned)
    received = [lax.all_to_all(first_rows, ("x", "z"), 0, 0, tiled=True)]
    later_rows = pl.pallas_call(
        later_kernel,
        out_shape=tuple(sds((size, quarter), BF16) for size in sizes[1:]),
        in_specs=[SMEM] + [VMEM] * 2,
        out_specs=(VMEM,) * (len(CHUNKS) - 1),
        compiler_params=params(16),
        cost_estimate=cost(2 * count * sum(sizes) * quarter, sum(sizes) * quarter * 2),
    )(pos, part, turned)
    arrays = (w_gate, w_up, w_down)
    sent, own = [
        [lax.dynamic_index_in_dim(array, core, 0, keepdims=False) for array in arrays]
        for core in (1 - pos[1], pos[1])
    ]
    *sent, received[0] = lax.optimization_barrier((*sent, received[0]))
    *own, received[0] = lax.optimization_barrier((*own, received[0]))
    others = [lax.ppermute(array, "c", [(0, 1), (1, 0)]) for array in sent]
    for rows in later_rows:
        rows, received[-1] = lax.optimization_barrier((rows, received[-1]))
        received.append(lax.all_to_all(rows, ("x", "z"), 0, 0, tiled=True))
    tokens, router, received[0] = lax.optimization_barrier((tokens, router, received[0]))
    mixes = pl.pallas_call(
        mix_kernel,
        out_shape=tuple(sds((count, size), BF16) for size in sizes),
        in_specs=[SMEM] + [VMEM] * 4,
        out_specs=(VMEM,) * len(CHUNKS),
        compiler_params=params(16),
        cost_estimate=cost(2 * count * width * 64, count * width * 2),
    )(pos, tokens, gain, router, turned)

    returned = []
    done = []
    for index, size in enumerate(sizes):
        mine = received[index]
        if index:
            before = [done[i][j] for i, j in ((index - 1, 0), (index - 2, 1)) if i >= 0]
            mine, *before = lax.optimization_barrier((mine, *before))
        blocks = lax.all_gather(mine, "y", axis=0)
        pieces = []
        for half in range(size // PIECE):
            if index == 1 and half == 0:
                blocks, returned[0] = lax.optimization_barrier((blocks, returned[0]))
            hidden = pl.pallas_call(
                functools.partial(hidden_kernel, half),
                out_shape=sds((PIECE, units), BF16),
                in_specs=[SMEM] + [VMEM] * 3 + [pl.BlockSpec(memory_space=pl.ANY)] * 2,
                out_specs=VMEM,
                scratch_shapes=[pltpu.VMEM((units // 2, width), BF16)] * 2
                + [pltpu.SemaphoreType.DMA((2,))],
                compiler_params=params(16),
                cost_estimate=cost(
                    4 * PIECE * width * units, 4 * units * width + 2 * PIECE * width
                ),
            )(pos, blocks, own[0], own[1], others[0], others[1])
            if index:
                pieces.extend(ring(hidden))
            else:
                pieces.append(lax.all_gather(hidden, "y", axis=0))
        result = pl.pallas_call(
            down_ring_kernel if index else down_kernel,
            out_shape=sds((size, NC * cols), BF16),
            in_specs=[SMEM] + [VMEM] * (2 + len(pieces)),
            out_specs=VMEM,
            compiler_params=params(16),
            cost_estimate=cost(
                2 * size * ff * NC * cols, 2 * ff * NC * cols + 2 * size * NC * cols
            ),
        )(pos, own[2], others[2], *pieces)
        if index == 0:
            result, received[-1] = lax.optimization_barrier((result, received[-1]))
        done.append((blocks, result))
        returned.append(lax.all_to_all(result, ("x", "z"), 0, 0, tiled=True))

    total = None
    last = len(CHUNKS) - 1
    for group in (range(last), range(last, last + 1)):
        keep, give = pl.pallas_call(
            combine_kernel,
            out_shape=(sds((count, cols), F32), sds((count, cols), BF16)),
            in_specs=[SMEM] + [VMEM] * (2 * len(group)),
            out_specs=(VMEM, VMEM),
            compiler_params=params(16),
            cost_estimate=cost(4 * count * cols * 512, 1 << 20),
        )(pos, *[item for i in group for item in (mixes[i], returned[i])])
        give = lax.ppermute(give, "c", [(0, 1), (1, 0)])
        share = keep + give.astype(F32)
        total = share if total is None else total + share
    return total.astype(BF16)


def solution(mesh):
    grid = Mesh(mesh.devices.reshape(NY, NC, NX, NZ), ("y", "c", "x", "z"))
    enc, exp = ("y", "c"), ("x", "z")
    return jax.shard_map(
        body,
        mesh=grid,
        in_specs=(
            P(exp, None),
            P(),
            P(),
            P(exp, None),
            P(exp, enc, None),
            P(exp, enc, None),
            P(exp, None, enc),
        ),
        out_specs=P(exp, enc),
        check_vma=False,
    )
```

```python
import functools

import jax
import jax.numpy as jnp
from jax import lax
from jax.experimental import pallas as pl
from jax.experimental.pallas import tpu as pltpu
from jax.sharding import Mesh, PartitionSpec as P

EPS = 1e-06
F32 = jnp.float32
BF16 = jnp.bfloat16
NY, NC, NX, NZ = 4, 2, 4, 8
N_EXP = NX * NZ
CHUNKS = ((0, 8), (8, 16), (24, 8))
PIECE = 256

VMEM = pl.BlockSpec(memory_space=pltpu.VMEM)
SMEM = pl.BlockSpec(memory_space=pltpu.SMEM)


def by_rows(left, right):
    return lax.dot_general(
        left, right, (((1,), (1,)), ((), ())), preferred_element_type=F32
    )


def times(left, right):
    return jnp.dot(left, right, preferred_element_type=F32)


def params(mib):
    return pltpu.CompilerParams(vmem_limit_bytes=mib << 20)


def cost(flops, moved):
    return pl.CostEstimate(flops=flops, bytes_accessed=moved, transcendentals=0)


def places(names, core):
    tokens = names.shape[1]
    expert = core.astype(F32) + 2.0 * lax.broadcasted_iota(
        jnp.int32, (N_EXP, tokens), 0
    ).astype(F32)
    hits = [names[k : k + 1, :] == expert for k in range(8)]
    named = hits[0]
    for hit in hits[1:]:
        named = named | hit
    row = lax.broadcasted_iota(jnp.int32, (tokens, tokens), 0)
    col = lax.broadcasted_iota(jnp.int32, (tokens, tokens), 1)
    earlier = jnp.where(row < col, 1.0, 0.0).astype(BF16)
    before = times(jnp.where(named, 1.0, 0.0).astype(BF16), earlier)
    return hits, jnp.where(named, before, -1.0)


def spread(place, values, first, size):
    tokens = place.shape[1]
    slot = lax.broadcasted_iota(jnp.int32, (size, tokens), 0) + first
    slot = slot.astype(F32)
    return jnp.concatenate(
        [
            jnp.where(place[d : d + 1, :] == slot, values[d : d + 1, :], 0.0)
            for d in range(N_EXP)
        ],
        axis=0,
    )


def pick(names, part, chunk, core):
    _, place = places(names, core)
    picks = spread(place, jnp.ones_like(place), *chunk).astype(BF16)
    return times(picks, part).astype(BF16)


def first_kernel(pos, tokens, gain, routes, part_out, rows_out):
    values = tokens[...].astype(F32)
    count, width = values.shape
    squares = jnp.sum(values * values, axis=1, keepdims=True)
    inverse = lax.rsqrt(squares / width + EPS)
    quarter = width // NY
    cols = pl.ds(pl.multiple_of(pos[0] * quarter, quarter), quarter)
    mine = (tokens[:, cols].astype(F32) * gain[:, cols].astype(F32)).astype(BF16)
    part = (mine.astype(F32) * inverse).astype(BF16)
    part_out[...] = part
    rows_out[...] = pick(routes[...].astype(F32), part, CHUNKS[0], pos[1])


def later_kernel(pos, part, routes, *rows_out):
    for chunk, out in zip(CHUNKS[1:], rows_out):
        out[...] = pick(routes[...].astype(F32), part[...], chunk, pos[1])


def mix_kernel(pos, tokens, gain, router, routes, *mix_out):
    values = tokens[...].astype(F32)
    count, width = values.shape
    scaled = (values * gain[...].astype(F32)).astype(BF16)
    squares = jnp.sum(values * values, axis=1, keepdims=True)
    inverse = lax.rsqrt(squares / width + EPS)
    turned = jnp.transpose(jnp.broadcast_to(inverse, (count, 128)))
    logits = by_rows(router[...], scaled) * turned[0:1, :]
    expert = lax.broadcasted_iota(jnp.int32, logits.shape, 0).astype(F32)
    names = routes[...].astype(F32)
    chosen = [
        jnp.sum(jnp.where(names[k : k + 1, :] == expert, logits, 0.0), axis=0, keepdims=True)
        for k in range(8)
    ]
    raised = jnp.exp(jnp.concatenate(chosen, axis=0))
    weights = raised / jnp.sum(raised, axis=0, keepdims=True)
    hits, place = places(names, pos[1])
    dense = jnp.zeros_like(place)
    for k in range(8):
        dense = dense + jnp.where(hits[k], weights[k : k + 1, :], 0.0)
    for (first, size), out in zip(CHUNKS, mix_out):
        out[...] = jnp.transpose(spread(place, dense, first, size)).astype(BF16)


def activate(pos, sums):
    units = sums.shape[0] // 4
    gate_own, up_own, gate_other, up_other = [
        sums[index * units : (index + 1) * units] for index in range(4)
    ]
    own = gate_own / (1.0 + jnp.exp(-gate_own)) * up_own
    other = gate_other / (1.0 + jnp.exp(-gate_other)) * up_other
    low = jnp.where(pos[1] == 0, own, other)
    high = jnp.where(pos[1] == 0, other, own)
    return jnp.transpose(jnp.concatenate([low, high], axis=0)).astype(BF16)


def hidden_kernel(
    half, pos, blocks, gate_own, gate_other, up_own, up_other, out, held, sems
):
    rows = pl.ds(half * PIECE, PIECE)
    fetches = [
        pltpu.make_async_copy(blocks.at[y, rows, :], held.at[y], sems.at[y]) for y in range(NY)
    ]
    for fetch in fetches:
        fetch.start()
    quarter = held.shape[2]
    total = None
    for y in range(NY):
        cols = slice(y * quarter, (y + 1) * quarter)
        weights = jnp.concatenate(
            [weight[:, cols] for weight in (gate_own, up_own, gate_other, up_other)], axis=0
        )
        fetches[y].wait()
        term = by_rows(weights, held[y])
        total = term if y == 0 else total + term
    out[...] = activate(pos, total)


def store_columns(pos, out, at, own, other):
    cols = own.shape[1]
    for core, total in ((pos[1], own), (1 - pos[1], other)):
        out[at, pl.ds(pl.multiple_of(core * cols, cols), cols)] = total.astype(BF16)


def down_ring_kernel(pos, down_own, down_other, *refs):
    out = refs[-1]
    for index in range(len(refs) // 5):
        own, low, high, far_top, far_bottom = refs[5 * index : 5 * index + 5]
        rows, units = own.shape
        far = jnp.concatenate([far_top[...], far_bottom[...]], axis=0)
        mine = theirs = None
        for block, step in ((own[...], 0), (low[...], 3), (high[...], 1), (far, 2)):
            at = lax.rem(pos[0] + step, NY)
            span = pl.ds(pl.multiple_of(at * units, units), units)
            own_term = times(block, down_own[span, :])
            other_term = times(block, down_other[span, :])
            mine = own_term if mine is None else mine + own_term
            theirs = other_term if theirs is None else theirs + other_term
        store_columns(pos, out, slice(index * rows, (index + 1) * rows), mine, theirs)


def combine_kernel(pos, *refs):
    keep_out, give_out = refs[-2:]
    cols = keep_out.shape[1]
    pairs = len(refs) // 2 - 1
    for out, core in ((give_out, 1 - pos[1]), (keep_out, pos[1])):
        at = pl.ds(pl.multiple_of(core * cols, cols), cols)
        total = None
        for index in range(pairs):
            step = times(refs[2 * index][...], refs[2 * index + 1][:, at])
            total = step if total is None else total + step
        out[...] = total.astype(out.dtype)


def turn(array, step):
    return lax.ppermute(array, "y", [(i, (i + step) % NY) for i in range(NY)])


def ring(block):
    half = block.shape[0] // 2
    low = turn(block, 1)
    high = turn(block, -1)
    return block, low, high, turn(low[:half], 1), turn(high[half:], -1)


def body(tokens, norm_gain, router, routes, w_gate, w_up, w_down):
    count, width = tokens.shape
    quarter = width // NY
    units = 2 * w_gate.shape[1]
    ff = w_down.shape[1]
    cols = w_down.shape[2]
    sds = jax.ShapeDtypeStruct
    pos = jnp.stack([lax.axis_index("y"), lax.axis_index("c")]).astype(jnp.int32)
    turned = routes.T
    sizes = [N_EXP * size for _, size in CHUNKS]

    gain = norm_gain[None, :]
    part, first_rows = pl.pallas_call(
        first_kernel,
        out_shape=(sds((count, quarter), BF16), sds((sizes[0], quarter), BF16)),
        in_specs=[SMEM] + [VMEM] * 3,
        out_specs=(VMEM, VMEM),
        compiler_params=params(16),
        cost_estimate=cost(2 * count * sizes[0] * quarter, count * width * 2),
    )(pos, tokens, gain, turned)
    received = [lax.all_to_all(first_rows, ("x", "z"), 0, 0, tiled=True)]
    later_rows = pl.pallas_call(
        later_kernel,
        out_shape=tuple(sds((size, quarter), BF16) for size in sizes[1:]),
        in_specs=[SMEM] + [VMEM] * 2,
        out_specs=(VMEM,) * (len(CHUNKS) - 1),
        compiler_params=params(16),
        cost_estimate=cost(2 * count * sum(sizes) * quarter, sum(sizes) * quarter * 2),
    )(pos, part, turned)
    arrays = (w_gate, w_up, w_down)
    sent, own = [
        [lax.dynamic_index_in_dim(array, core, 0, keepdims=False) for array in arrays]
        for core in (1 - pos[1], pos[1])
    ]
    *sent, received[0] = lax.optimization_barrier((*sent, received[0]))
    *own, received[0] = lax.optimization_barrier((*own, received[0]))
    others = [lax.ppermute(array, "c", [(0, 1), (1, 0)]) for array in sent]
    for rows in later_rows:
        rows, received[-1] = lax.optimization_barrier((rows, received[-1]))
        received.append(lax.all_to_all(rows, ("x", "z"), 0, 0, tiled=True))
    tokens, router, received[0] = lax.optimization_barrier((tokens, router, received[0]))
    mixes = pl.pallas_call(
        mix_kernel,
        out_shape=tuple(sds((count, size), BF16) for size in sizes),
        in_specs=[SMEM] + [VMEM] * 4,
        out_specs=(VMEM,) * len(CHUNKS),
        compiler_params=params(16),
        cost_estimate=cost(2 * count * width * 64, count * width * 2),
    )(pos, tokens, gain, router, turned)

    returned = []
    done = []
    for index, size in enumerate(sizes):
        mine = received[index]
        if index:
            before = [done[i][j] for i, j in ((index - 1, 0), (index - 2, 1)) if i >= 0]
            mine, *before = lax.optimization_barrier((mine, *before))
        blocks = lax.all_gather(mine, "y", axis=0)
        if index == 1:
            blocks, returned[0] = lax.optimization_barrier((blocks, returned[0]))
        pieces = []
        for half in range(size // PIECE):
            hidden = pl.pallas_call(
                functools.partial(hidden_kernel, half),
                out_shape=sds((PIECE, units), BF16),
                in_specs=[SMEM, pl.BlockSpec(memory_space=pltpu.HBM)] + [VMEM] * 4,
                out_specs=VMEM,
                scratch_shapes=[
                    pltpu.VMEM((NY, PIECE, quarter), BF16),
                    pltpu.SemaphoreType.DMA((NY,)),
                ],
                compiler_params=params(50),
                cost_estimate=cost(
                    4 * PIECE * width * units, 4 * units * width + 2 * PIECE * width
                ),
            )(pos, blocks, own[0], others[0], own[1], others[1])
            pieces.extend(ring(hidden))
        result = pl.pallas_call(
            down_ring_kernel,
            out_shape=sds((size, NC * cols), BF16),
            in_specs=[SMEM] + [VMEM] * (2 + len(pieces)),
            out_specs=VMEM,
            compiler_params=params(16),
            cost_estimate=cost(
                2 * size * ff * NC * cols, 2 * ff * NC * cols + 2 * size * NC * cols
            ),
        )(pos, own[2], others[2], *pieces)
        if index == 0:
            result, received[-1] = lax.optimization_barrier((result, received[-1]))
        done.append((blocks, result))
        returned.append(lax.all_to_all(result, ("x", "z"), 0, 0, tiled=True))

    total = None
    last = len(CHUNKS) - 1
    for group in (range(last), range(last, last + 1)):
        keep, give = pl.pallas_call(
            combine_kernel,
            out_shape=(sds((count, cols), F32), sds((count, cols), BF16)),
            in_specs=[SMEM] + [VMEM] * (2 * len(group)),
            out_specs=(VMEM, VMEM),
            compiler_params=params(16),
            cost_estimate=cost(4 * count * cols * 512, 1 << 20),
        )(pos, *[item for i in group for item in (mixes[i], returned[i])])
        give = lax.ppermute(give, "c", [(0, 1), (1, 0)])
        share = keep + give.astype(F32)
        total = share if total is None else total + share
    return total.astype(BF16)


def solution(mesh):
    grid = Mesh(mesh.devices.reshape(NY, NC, NX, NZ), ("y", "c", "x", "z"))
    enc, exp = ("y", "c"), ("x", "z")
    return jax.shard_map(
        body,
        mesh=grid,
        in_specs=(
            P(exp, None),
            P(),
            P(),
            P(exp, None),
            P(exp, enc, None),
            P(exp, enc, None),
            P(exp, None, enc),
        ),
        out_specs=P(exp, enc),
        check_vma=False,
    )
```
